128 devices in a mesh: px: 8 (over x, core), py: 16 (over z, y).
Axes of the slice: x: 4, y: 4, z: 4, core: 2. Of those that a mesh axis runs over, the one named last changes fastest.
Arguments:
- conserved: float32 [5, 6, 6, 6, 16384], P(None, None, None, None, ('px', 'py')), may hold values from -1 to 5, as said below
- flow_lists: int32 [128, 2, 32], P(('px', 'py')), may hold values from 0 to 127, as said below
- span_lists: int32 [128, 2, 64], P(('px', 'py')), may hold values from 0 to 127, as said below
- face_source: int32 [6, 16384], P(None, ('px', 'py')), may hold values from 0 to 1727, as said below
Outputs:
- advanced: float32 [5, 6, 6, 6, 16384], P(None, None, None, None, ('px', 'py'))
- register: float32 [5, 6, 6, 6, 16384], P(None, None, None, None, ('px', 'py'))
The draws below stay inside these ranges and needn't reach their ends.
Inputs may be any that keep to these rules, and one draw needn't show every extreme that they name: `conserved`: density lies in 0.7 to 1.3, each velocity component within 0.75 in magnitude, pressure in 0.55 to 1.45. Entry k of flow_lists[d, 0] (of flow_lists[d, 1]) is the slot of the element whose side 0 (side 1) carries the k-th face of the block boundary toward the block one lower (one higher) along the flow, cyclically; the receiving block lists its matching faces in the same order. Every block boundary along the flow has 32 faces. Entry k of span_lists[d, 0] (of span_lists[d, 1]) is the slot of the element whose side 4 (side 5) carries the k-th face of the block boundary toward the block one lower (one higher) along the span, cyclically, in the order shared with that block; a block boundary has at most 64 faces, some boundary has exactly 64, and entries past a boundary's faces hold 0. `face_source`: columns of the table described in the reference program. Sides 2 and 3 at the channel walls point at the wall values; slots outside a device's live block point at wall values on all six sides; every other side points at the side of the element that shares its face, which points back.
All inputs are finite; a program needn't handle non-finite values.
Results may differ from the reference program's by a relative error of at most 0.0003.
Values sent between devices are 32-bit elements; how exact they have to be, the bound alone decides.
No kernel may reach another device: no remote copies, remote signals or barrier semaphores. Data moves between devices by JAX's collectives and lax.ppermute only.
A program may use at most 192 MiB of HBM per device.

```python
import math
import jax
import jax.numpy as jnp
import numpy as np
from jax import lax

NP = 6
BY = 16
BZ = 2
BXMAX = 4
SECTIONS = 5
E_DEV = 128
CAPX = 32
CAPZ = 64
ELEMENTS = 16384
N_PX = 8
N_PY = 16


GAMMA = 1.4


def mesh_tables(key):
    width_key, full_key, half_key, order_key = jax.random.split(key, 4)
    device_count = N_PX * N_PY
    narrow = max(1, BXMAX // 2)
    widths = jax.random.randint(width_key, (N_PX,), narrow, BXMAX + 1)
    full_column = jax.random.randint(full_key, (), 0, N_PX)
    half_column = (full_column + 1 + jax.random.randint(half_key, (), 0, max(N_PX - 1, 1))) % N_PX
    columns = jnp.arange(N_PX)
    widths = jnp.where(columns == half_column, narrow, widths)
    widths = jnp.where(columns == full_column, BXMAX, widths)
    orders = jax.vmap(lambda sub_key: jax.random.permutation(sub_key, E_DEV))(jax.random.split(order_key, device_count)).astype(jnp.int32)
    linear = jnp.arange(E_DEV)
    pos_x = linear // (BY * BZ)
    pos_y = linear // BZ % BY
    pos_z = linear % BZ
    width = widths[jnp.arange(device_count) // N_PY][:, None]
    live = pos_x[None, :] < width

    def slot_at(coord_x, coord_y, coord_z):
        place = (jnp.clip(coord_x, 0, BXMAX - 1) * BY + jnp.clip(coord_y, 0, BY - 1)) * BZ + jnp.clip(coord_z, 0, BZ - 1)
        place = jnp.broadcast_to(place, (device_count, place.shape[-1]))
        return jnp.take_along_axis(orders, place, axis=1)
    own_slot = orders
    base = 6 * E_DEV
    walls = base + 2 * CAPX + 2 * CAPZ
    flow_index = pos_y * BZ + pos_z
    span_index = pos_x * BY + pos_y
    side_zero = jnp.where(pos_x[None, :] > 0, E_DEV + slot_at(pos_x - 1, pos_y, pos_z), base + CAPX + flow_index[None, :])
    side_one = jnp.where(pos_x[None, :] < width - 1, slot_at(pos_x + 1, pos_y, pos_z), base + flow_index[None, :])
    side_two = jnp.where(pos_y[None, :] > 0, 3 * E_DEV + slot_at(pos_x, pos_y - 1, pos_z), walls + 2 * E_DEV + own_slot)
    side_three = jnp.where(pos_y[None, :] < BY - 1, 2 * E_DEV + slot_at(pos_x, pos_y + 1, pos_z), walls + 3 * E_DEV + own_slot)
    side_four = jnp.where(pos_z[None, :] > 0, 5 * E_DEV + slot_at(pos_x, pos_y, pos_z - 1), base + 2 * CAPX + CAPZ + span_index[None, :])
    side_five = jnp.where(pos_z[None, :] < BZ - 1, 4 * E_DEV + slot_at(pos_x, pos_y, pos_z + 1), base + 2 * CAPX + span_index[None, :])
    sides = [side_zero, side_one, side_two, side_three, side_four, side_five]
    sides = [jnp.where(live, sides[side_index], walls + side_index * E_DEV + own_slot) for side_index in range(6)]
    by_linear = jnp.stack(sides, axis=1)
    inverse = jnp.argsort(orders, axis=1).astype(jnp.int32)
    by_slot = jnp.take_along_axis(by_linear, jnp.broadcast_to(inverse[:, None, :], by_linear.shape), axis=2)
    face_source = by_slot.transpose(1, 0, 2).reshape(6, device_count * E_DEV)
    flow_k = jnp.arange(CAPX)
    flow_first = slot_at(jnp.zeros_like(flow_k), flow_k // BZ, flow_k % BZ)
    flow_second = slot_at(width - 1, flow_k // BZ, flow_k % BZ)
    flow_lists = jnp.stack([flow_first, flow_second], axis=1)
    span_k = jnp.arange(CAPZ)
    valid = (span_k // BY)[None, :] < width
    span_first = jnp.where(valid, slot_at(span_k // BY, span_k % BY, jnp.zeros_like(span_k)), 0)
    span_second = jnp.where(valid, slot_at(span_k // BY, span_k % BY, jnp.full_like(span_k, BZ - 1)), 0)
    span_lists = jnp.stack([span_first, span_second], axis=1)
    return (flow_lists.astype(jnp.int32), span_lists.astype(jnp.int32), face_source.astype(jnp.int32))


def draw_flow_lists(key, part):
    return mesh_tables(key)[0]


def draw_span_lists(key, part):
    return mesh_tables(key)[1]


def draw_face_source(key, part):
    return mesh_tables(key)[2]


def draw_conserved(key, part):
    key = jax.random.fold_in(key, 7)
    density_key, velocity_key, pressure_key = jax.random.split(key, 3)
    shaped = (NP, NP, NP, ELEMENTS)
    density = 1.0 + 0.1 * jnp.clip(jax.random.normal(density_key, shaped, jnp.float32), -3.0, 3.0)
    velocity = 0.25 * jnp.clip(jax.random.normal(velocity_key, (3,) + shaped, jnp.float32), -3.0, 3.0)
    pressure = 1.0 + 0.15 * jnp.clip(jax.random.normal(pressure_key, shaped, jnp.float32), -3.0, 3.0)
    energy = pressure / (GAMMA - 1.0) + 0.5 * density * jnp.sum(velocity * velocity, axis=0)
    return jnp.concatenate([density[None], density[None] * velocity, energy[None]], axis=0).astype(jnp.float32)


def setup_inputs(seed: int = 0) -> dict:
    key_of = jax.random.split(jax.random.key(seed), 5)
    conserved = draw_conserved(jax.random.fold_in(key_of[4], 71), 0)
    flow_lists = draw_flow_lists(jax.random.fold_in(key_of[4], 71), 0)
    span_lists = draw_span_lists(jax.random.fold_in(key_of[4], 71), 0)
    face_source = draw_face_source(jax.random.fold_in(key_of[4], 71), 0)
    return dict(conserved=conserved, flow_lists=flow_lists, span_lists=span_lists, face_source=face_source)


GAMMA = 1.4
VISCOSITY = 0.02
TIME_STEP = 0.01
RK_A = (0.0, -567301805773.0 / 1357537059087.0, -2404267990393.0 / 2016746695238.0, -3550918686646.0 / 2091501179385.0, -1275806237668.0 / 842570457699.0)
RK_B = (1432997174477.0 / 9575080441755.0, 5161836677717.0 / 13612068292357.0, 1720146321549.0 / 2090206949498.0, 3134564353537.0 / 4481467310338.0, 2277821191437.0 / 14882151754819.0)
VOLUME_FORMS = ('xy,vxyjkz->vxjkz', 'xy,vixykz->vixkz', 'xy,vijxyz->vijxz')
DERIVE_FORMS = ('xy,vyjkz->vxjkz', 'xy,viykz->vixkz', 'xy,vijyz->vijxz')
MOMENTUM_SIGN = (1.0, -1.0, -1.0, -1.0, 1.0)

def lobatto_tables():
    inner_node = math.sqrt(1.0 / 3.0 - 2.0 * math.sqrt(7.0) / 21.0)
    outer_node = math.sqrt(1.0 / 3.0 + 2.0 * math.sqrt(7.0) / 21.0)
    points = np.array([-1.0, -outer_node, -inner_node, inner_node, outer_node, 1.0])
    legendre = (63.0 * points ** 5 - 70.0 * points ** 3 + 15.0 * points) / 8.0
    weights = 2.0 / (30.0 * legendre * legendre)
    identity = np.eye(6)
    differences = points[:, None] - points[None, :] + identity
    barycentric = 1.0 / np.prod(differences, axis=1)
    matrix = barycentric[None, :] / barycentric[:, None] / differences
    matrix = matrix * (1.0 - identity)
    matrix = matrix - identity * np.sum(matrix, axis=1)[:, None]
    lift_left = np.zeros(6)
    lift_left[0] = 1.0 / weights[0]
    lift_right = np.zeros(6)
    lift_right[5] = 1.0 / weights[5]
    return (jnp.asarray(matrix, jnp.float32), jnp.asarray(lift_left, jnp.float32), jnp.asarray(lift_right, jnp.float32))

def primitive(conserved):
    density = conserved[0]
    velocity = (conserved[1] / density, conserved[2] / density, conserved[3] / density)
    kinetic = velocity[0] * velocity[0] + velocity[1] * velocity[1] + velocity[2] * velocity[2]
    pressure = (GAMMA - 1.0) * (conserved[4] - 0.5 * density * kinetic)
    return (density, velocity, pressure, conserved[4] / density)

def two_point(left_states, right_states, direction):
    density = 0.5 * (left_states[0] + right_states[0])
    velocity = tuple((0.5 * (left_states[1][comp_index] + right_states[1][comp_index]) for comp_index in range(3)))
    pressure = 0.5 * (left_states[2] + right_states[2])
    specific = 0.5 * (left_states[3] + right_states[3])
    mass_flux = density * velocity[direction]
    momentum = [mass_flux * velocity[comp_index] for comp_index in range(3)]
    momentum[direction] = momentum[direction] + pressure
    energy = mass_flux * specific + pressure * velocity[direction]
    return jnp.stack([mass_flux, momentum[0], momentum[1], momentum[2], energy])

def physical(conserved, direction):
    states = primitive(conserved)
    return two_point(states, states, direction)

def rusanov(left_cons, right_cons, direction):
    left_states = primitive(left_cons)
    right_states = primitive(right_cons)
    left_speed = jnp.abs(left_states[1][direction]) + jnp.sqrt(GAMMA * left_states[2] / left_states[0])
    right_speed = jnp.abs(right_states[1][direction]) + jnp.sqrt(GAMMA * right_states[2] / right_states[0])
    wave_speed = jnp.maximum(left_speed, right_speed)
    average = 0.5 * (two_point(left_states, left_states, direction) + two_point(right_states, right_states, direction))
    return average - 0.5 * wave_speed * (right_cons - left_cons)

def volume_term(conserved, matrix):
    states = primitive(conserved)
    summed = None
    for direction in range(3):
        left_states = jax.tree.map(lambda leaf_value: jnp.expand_dims(leaf_value, direction + 1), states)
        right_states = jax.tree.map(lambda leaf_value: jnp.expand_dims(leaf_value, direction), states)
        fluxes = two_point(left_states, right_states, direction)
        contribution = jnp.einsum(VOLUME_FORMS[direction], 2.0 * matrix, fluxes, precision=lax.Precision.HIGHEST)
        summed = contribution if summed is None else summed + contribution
    return summed

def derivative(node_field, direction, matrix):
    return jnp.einsum(DERIVE_FORMS[direction], matrix, node_field, precision=lax.Precision.HIGHEST)

def side_trace(node_field, side_index):
    last_node = node_field.shape[1] - 1
    position = 0 if side_index % 2 == 0 else last_node
    face_values = lax.index_in_dim(node_field, position, side_index // 2 + 1, keepdims=False)
    return face_values.reshape(node_field.shape[0], -1, node_field.shape[-1])

def face_traces(node_field):
    return jnp.stack([side_trace(node_field, side_index) for side_index in range(6)], axis=2)

def normal_traces(gradients):
    return jnp.stack([side_trace(gradients[side_index // 2], side_index) for side_index in range(6)], axis=2)

def add_surface(node_field, correction, direction, lift_left, lift_right):
    var_count, node_count = (node_field.shape[0], node_field.shape[1])
    slot_count = node_field.shape[-1]
    shaped = [1, 1, 1, 1, 1]
    shaped[direction + 1] = node_count
    even_side = correction[:, :, 2 * direction].reshape(var_count, node_count, node_count, slot_count)
    odd_side = correction[:, :, 2 * direction + 1].reshape(var_count, node_count, node_count, slot_count)
    node_field = node_field - jnp.expand_dims(even_side, direction + 1) * lift_left.reshape(shaped)
    return node_field + jnp.expand_dims(odd_side, direction + 1) * lift_right.reshape(shaped)

def neighbours(own_traces, wall_traces, flow_lists, span_lists, face_source):
    var_count, node_rows, side_count, element_count = own_traces.shape
    device_count = N_PX * N_PY
    slot_count = E_DEV

    def per_device(node_field):
        shaped = node_field.reshape(var_count, node_rows, side_count, device_count, slot_count)
        return shaped.transpose(0, 1, 3, 2, 4).reshape(var_count, node_rows, device_count, side_count * slot_count)

    def device_take(table_part, slot_lists):
        return jax.vmap(lambda table_one, ids_one: jnp.take(table_one, ids_one, axis=2), in_axes=(2, 0), out_axes=2)(table_part, slot_lists)

    def roll_grid(lists_part, offset, grid_axis):
        shaped = lists_part.reshape(var_count, node_rows, N_PX, N_PY, lists_part.shape[-1])
        return jnp.roll(shaped, offset, axis=grid_axis).reshape(lists_part.shape)
    local_table = per_device(own_traces)
    first_flow = device_take(local_table, flow_lists[:, 0])
    second_flow = device_take(local_table, slot_count + flow_lists[:, 1])
    first_span = device_take(local_table, 4 * slot_count + span_lists[:, 0])
    second_span = device_take(local_table, 5 * slot_count + span_lists[:, 1])
    full_table = jnp.concatenate([local_table, roll_grid(first_flow, -1, 2), roll_grid(second_flow, 1, 2), roll_grid(first_span, -1, 3), roll_grid(second_span, 1, 3), per_device(wall_traces)], axis=3)
    columns = face_source.reshape(side_count, device_count, slot_count).transpose(1, 0, 2).reshape(device_count, side_count * slot_count)
    gathered = device_take(full_table, columns)
    gathered = gathered.reshape(var_count, node_rows, device_count, side_count, slot_count)
    return gathered.transpose(0, 1, 3, 2, 4).reshape(own_traces.shape)

def volume_blocks(conserved, matrix):
    blocks = jnp.moveaxis(conserved.reshape(conserved.shape[:4] + (N_PX * N_PY, E_DEV)), 4, 0)
    mapped = lax.map(lambda element_block: volume_term(element_block, matrix), blocks)
    return jnp.moveaxis(mapped, 0, 4).reshape(conserved.shape)

def time_rate(conserved, flow_lists, span_lists, face_source):
    matrix, lift_left, lift_right = lobatto_tables()
    signs = jnp.array(MOMENTUM_SIGN, jnp.float32)[:, None, None, None]
    own_solution = face_traces(conserved)
    other_solution = neighbours(own_solution, own_solution * signs, flow_lists, span_lists, face_source)
    solution_jump = 0.5 * (own_solution + other_solution) - own_solution
    gradients = [add_surface(derivative(conserved, direction, matrix), solution_jump, direction, lift_left, lift_right) for direction in range(3)]
    normal_own = normal_traces(gradients)
    normal_other = neighbours(normal_own, normal_own, flow_lists, span_lists, face_source)
    gradient_jump = 0.5 * (normal_own + normal_other) - normal_own
    viscous = None
    for direction in range(3):
        contribution = add_surface(derivative(gradients[direction], direction, matrix), gradient_jump, direction, lift_left, lift_right)
        viscous = contribution if viscous is None else viscous + contribution
    corrections = []
    for side_index in range(6):
        direction = side_index // 2
        own_side = own_solution[:, :, side_index]
        other_side = other_solution[:, :, side_index]
        if side_index % 2 == 1:
            riemann = rusanov(own_side, other_side, direction)
        else:
            riemann = rusanov(other_side, own_side, direction)
        corrections.append(riemann - physical(own_side, direction))
    correction = jnp.stack(corrections, axis=2)
    advective = volume_blocks(conserved, matrix)
    for direction in range(3):
        advective = add_surface(advective, correction, direction, lift_left, lift_right)
    return VISCOSITY * viscous - advective

def reference(conserved, flow_lists, span_lists, face_source):
    register = jnp.zeros_like(conserved)
    for section_index in range(SECTIONS):
        rate = time_rate(conserved, flow_lists, span_lists, face_source)
        register = RK_A[section_index] * register + TIME_STEP * rate
        conserved = conserved + RK_B[section_index] * register
    return (conserved, register)
```

```python
import math

import jax
import jax.numpy as jnp
import numpy as np
from jax import lax
from jax.experimental import pallas as pl
from jax.experimental.pallas import tpu as pltpu
from jax.sharding import PartitionSpec as P

GAMMA = 1.4
VISCOSITY = 0.02
TIME_STEP = 0.01
RK_A = (
    0.0,
    -567301805773.0 / 1357537059087.0,
    -2404267990393.0 / 2016746695238.0,
    -3550918686646.0 / 2091501179385.0,
    -1275806237668.0 / 842570457699.0,
)
RK_B = (
    1432997174477.0 / 9575080441755.0,
    5161836677717.0 / 13612068292357.0,
    1720146321549.0 / 2090206949498.0,
    3134564353537.0 / 4481467310338.0,
    2277821191437.0 / 14882151754819.0,
)


def lobatto_tables():
    inner_node = math.sqrt(1.0 / 3.0 - 2.0 * math.sqrt(7.0) / 21.0)
    outer_node = math.sqrt(1.0 / 3.0 + 2.0 * math.sqrt(7.0) / 21.0)
    points = np.array([-1.0, -outer_node, -inner_node, inner_node, outer_node, 1.0])
    legendre = (63.0 * points**5 - 70.0 * points**3 + 15.0 * points) / 8.0
    weights = 2.0 / (30.0 * legendre * legendre)
    identity = np.eye(6)
    differences = points[:, None] - points[None, :] + identity
    barycentric = 1.0 / np.prod(differences, axis=1)
    matrix = barycentric[None, :] / barycentric[:, None] / differences
    matrix = matrix * (1.0 - identity)
    matrix = matrix - identity * np.sum(matrix, axis=1)[:, None]
    return matrix, weights


DM, WEIGHTS = lobatto_tables()
DM2 = DM @ DM
LIFT = 1.0 / WEIGHTS[0]
NV = 5
VROWS = 320
FIELD = (NV * VROWS, 128)
FACE0 = (2, 60, 8, 128)
FACE2 = (2, 50, 8, 128)
FLOW_PACK = (15, 8, 128)
SPAN_PACK = (25, 8, 128)
CODES = (10, 8, 128)
RECEIVED = 256
WALL = 512


def tile_at(ref, row):
    return ref[pl.ds(pl.multiple_of(row, 8), 8), :]


def put_tile(ref, row, value):
    ref[pl.ds(pl.multiple_of(row, 8), 8), :] = value


def line_at(ref, var, chunk, k):
    return ref[pl.ds(var * VROWS + chunk * 64 + k, 8, stride=8), :]


def put_line(ref, var, chunk, k, value):
    ref[pl.ds(var * VROWS + chunk * 64 + k, 8, stride=8), :] = value


def take_lanes(value, index):
    return jnp.take_along_axis(value, index, axis=1, mode="promise_in_bounds")


def even_odd(values):
    even = [values[m] + values[5 - m] for m in range(3)]
    odd = [values[m] - values[5 - m] for m in range(3)]
    return even, odd


def combine(coefficients, terms):
    total = None
    for coefficient, term in zip(coefficients, terms):
        part = float(coefficient) * term
        total = part if total is None else total + part
    return total


def end_derivatives(values):
    even, odd = even_odd(values)
    first = combine([(DM[0, m] + DM[0, 5 - m]) / 2 for m in range(3)], even)
    second = combine([(DM[0, m] - DM[0, 5 - m]) / 2 for m in range(3)], odd)
    return first + second, second - first


def second_derivative(values, scale):
    even, odd = even_odd(values)
    result = [None] * 6
    for i in range(3):
        first = combine([scale * (DM2[i, m] + DM2[i, 5 - m]) / 2 for m in range(3)], even)
        second = combine([scale * (DM2[i, m] - DM2[i, 5 - m]) / 2 for m in range(3)], odd)
        result[i] = first + second
        result[5 - i] = first - second
    return result


def half_primitive(state):
    inverse = 1.0 / state[0]
    half = 0.5 * inverse
    velocity = [half * state[1], half * state[2], half * state[3]]
    kinetic = velocity[0] * state[1] + velocity[1] * state[2] + velocity[2] * state[3]
    pressure = (0.5 * (GAMMA - 1.0)) * (state[4] - kinetic)
    return [0.5 * state[0], velocity[0], velocity[1], velocity[2], pressure, half * state[4]]


def line_fluxes(nodes, direction):
    sums = [[None] * NV for _ in range(6)]

    def add(node, var, value, sign):
        old = sums[node][var]
        if old is None:
            sums[node][var] = value if sign > 0 else -value
        else:
            sums[node][var] = old + value if sign > 0 else old - value

    for i in range(6):
        for m in range(i + 1, 6):
            weight = float(2.0 * WEIGHTS[i] * DM[i, m])
            left, right = nodes[i], nodes[m]
            density, v0, v1, v2, pressure, specific = [left[n] + right[n] for n in range(6)]
            velocity = (v0, v1, v2)
            mass = (weight * density) * velocity[direction]
            scaled = weight * pressure
            flux = [mass, mass * v0, mass * v1, mass * v2, mass * specific + scaled * velocity[direction]]
            flux[1 + direction] = flux[1 + direction] + scaled
            for var in range(NV):
                add(i, var, flux[var], 1)
                add(m, var, flux[var], -1)
    return sums


def rusanov(left, right, direction):
    def parts(state):
        inverse = 1.0 / state[0]
        velocity = state[1 + direction] * inverse
        kinetic = state[1] * state[1] + state[2] * state[2] + state[3] * state[3]
        pressure = (GAMMA - 1.0) * (state[4] - 0.5 * inverse * kinetic)
        speed = jnp.abs(velocity) + jnp.sqrt(GAMMA * pressure * inverse)
        flux = [state[1 + direction], state[1] * velocity, state[2] * velocity, state[3] * velocity]
        flux.append((state[4] + pressure) * velocity)
        flux[1 + direction] = flux[1 + direction] + pressure
        return flux, speed

    left_flux, left_speed = parts(left)
    right_flux, right_speed = parts(right)
    speed = jnp.maximum(left_speed, right_speed)
    return [
        0.5 * ((left_flux[n] + right_flux[n]) - speed * (right[n] - left[n])) for n in range(NV)
    ]


def face_terms(low, high, direction):
    low_flux = rusanov(low[2], low[0], direction)
    high_flux = rusanov(high[0], high[2], direction)
    visc = 0.5 * VISCOSITY * LIFT
    end_low, end_high, jump_low, jump_high = [], [], [], []
    for n in range(NV):
        end_low.append(LIFT * low_flux[n] - visc * (low[3][n] - low[1][n]))
        end_high.append(visc * (high[3][n] - high[1][n]) - LIFT * high_flux[n])
        jump_low.append(visc * (low[2][n] - low[0][n]))
        jump_high.append(visc * (high[2][n] - high[0][n]))
    return end_low, end_high, jump_low, jump_high


def add_faces(values, terms, var, scale):
    end_low, end_high, jump_low, jump_high = terms
    result = []
    for i in range(6):
        value = values[i] + float(scale * DM[i, 5]) * jump_high[var] - float(scale * DM[i, 0]) * jump_low[var]
        if i == 0:
            value = value + scale * end_low[var]
        if i == 5:
            value = value + scale * end_high[var]
        result.append(value)
    return result


def make_faces(field, face0, face2):
    def flow_row(j, carry):
        for v in range(NV):
            values = [tile_at(field, v * VROWS + i * 48 + j * 8) for i in range(6)]
            first, last = end_derivatives(values)
            face0[0, v * 6 + j] = values[0]
            face0[1, v * 6 + j] = values[5]
            face0[0, (NV + v) * 6 + j] = first
            face0[1, (NV + v) * 6 + j] = last
        return carry

    lax.fori_loop(0, 6, flow_row, 0)

    def span_row(chunk, carry):
        for v in range(NV):
            values = [line_at(field, v, chunk, k) for k in range(6)]
            first, last = end_derivatives(values)
            face2[0, v * 5 + chunk] = values[0]
            face2[1, v * 5 + chunk] = values[5]
            face2[0, (NV + v) * 5 + chunk] = first
            face2[1, (NV + v) * 5 + chunk] = last
        return carry

    lax.fori_loop(0, 5, span_row, 0)


def pack_faces(parity, codes, face0, face2, flow_a, flow_b, span_a, span_b):
    lane = lax.broadcasted_iota(jnp.int32, (8, 128), 1)
    flow_odd, span_odd = parity[0], parity[1]
    for side, out in ((1 - flow_odd, flow_a), (flow_odd, flow_b)):
        index = codes[6 + side]
        for t in range(15):
            packed = take_lanes(face0[side, t], index)
            for g in range(1, 4):
                packed = jnp.where(lane >= 32 * g, take_lanes(face0[side, 15 * g + t], index), packed)
            out[t] = packed
    for side, out in ((1 - span_odd, span_a), (span_odd, span_b)):
        index = codes[8 + side]
        for t in range(25):
            out[t] = jnp.where(
                lane >= 64, take_lanes(face2[side, 25 + t], index), take_lanes(face2[side, t], index)
            )


def first_kernel(
    parity, conserved, lists, field, codes, face0, face2, flow_a, flow_b, span_a, span_b
):
    for v in range(NV):
        for i in range(6):
            for j in range(6):
                field[pl.ds(v * VROWS + i * 48 + j * 8, 6), :] = conserved[v, i, j]
    for side in range(6):
        column = lists[pl.ds(side, 1), :]
        mask = 31 if side < 2 else 63
        offset = 768 if side < 2 else 832
        code = jnp.where(
            column < 768,
            column & 127,
            jnp.where(column < 960, ((column - offset) & mask) + RECEIVED, WALL),
        )
        codes[side] = jnp.broadcast_to(code, (8, 128))
    for row in range(6, 10):
        codes[row] = jnp.broadcast_to(lists[pl.ds(row, 1), :], (8, 128))
    make_faces(field, face0, face2)
    pack_faces(parity, codes, face0, face2, flow_a, flow_b, span_a, span_b)


def volume_kernel(section, field, register, codes, face0, face2, base, near0, near2, prims):
    step = TIME_STEP

    def primitives(n, carry):
        for u in range(4):
            row = (n * 4 + u) * 8
            values = half_primitive([tile_at(field, v * VROWS + row) for v in range(NV)])
            for q in range(6):
                put_tile(prims, q * VROWS + row, values[q])
        return carry

    lax.fori_loop(0, 9, primitives, 0)

    def viscous_and_flux(lines, nodes, direction, var, sums):
        second = second_derivative(lines[var], step * VISCOSITY)
        return [second[i] - float(step / WEIGHTS[i]) * sums[i][var] for i in range(6)]

    def flow_row(j, carry):
        row = j * 8
        nodes = [[tile_at(prims, q * VROWS + i * 48 + row) for q in range(6)] for i in range(6)]
        sums = line_fluxes(nodes, 0)
        for v in range(NV):
            line = [tile_at(field, v * VROWS + i * 48 + row) for i in range(6)]
            second = second_derivative(line, step * VISCOSITY)
            for i in range(6):
                value = second[i] - float(step / WEIGHTS[i]) * sums[i][v]
                if section > 0:
                    value = value + RK_A[section] * tile_at(register, v * VROWS + i * 48 + row)
                put_tile(base, v * VROWS + i * 48 + row, value)
        return carry

    lax.fori_loop(0, 6, flow_row, 0)

    low_code, high_code = codes[2], codes[3]
    low_index, high_index = low_code & 127, high_code & 127
    low_wall, high_wall = low_code >= WALL, high_code >= WALL

    def wall_row(i, carry):
        row = i * 48
        nodes = [[tile_at(prims, q * VROWS + row + j * 8) for q in range(6)] for j in range(6)]
        sums = line_fluxes(nodes, 1)
        lines = [[tile_at(field, v * VROWS + row + j * 8) for j in range(6)] for v in range(NV)]
        ends = [end_derivatives(line) for line in lines]
        low = ([line[0] for line in lines], [end[0] for end in ends], [], [])
        high = ([line[5] for line in lines], [end[1] for end in ends], [], [])
        for v in range(NV):
            sign = -1.0 if 1 <= v <= 3 else 1.0
            low[2].append(jnp.where(low_wall, sign * low[0][v], take_lanes(high[0][v], low_index)))
            low[3].append(jnp.where(low_wall, low[1][v], take_lanes(high[1][v], low_index)))
            high[2].append(jnp.where(high_wall, sign * high[0][v], take_lanes(low[0][v], high_index)))
            high[3].append(jnp.where(high_wall, high[1][v], take_lanes(low[1][v], high_index)))
        terms = face_terms(low, high, 1)
        for v in range(NV):
            second = second_derivative(lines[v], step * VISCOSITY)
            values = [second[j] - float(step / WEIGHTS[j]) * sums[j][v] for j in range(6)]
            values = add_faces(values, terms, v, step)
            for j in range(6):
                where = v * VROWS + row + j * 8
                put_tile(base, where, tile_at(base, where) + values[j])
        return carry

    lax.fori_loop(0, 6, wall_row, 0)

    def span_row(chunk, carry):
        nodes = [[line_at(prims, q, chunk, k) for q in range(6)] for k in range(6)]
        sums = line_fluxes(nodes, 2)
        for v in range(NV):
            line = [line_at(field, v, chunk, k) for k in range(6)]
            second = second_derivative(line, step * VISCOSITY)
            for k in range(6):
                value = second[k] - float(step / WEIGHTS[k]) * sums[k][v]
                put_line(base, v, chunk, k, line_at(base, v, chunk, k) + value)
        return carry

    lax.fori_loop(0, 5, span_row, 0)

    for face, near, tiles, first_side in ((face0, near0, 6, 0), (face2, near2, 5, 4)):
        for side in range(2):
            code = codes[first_side + side]
            index, wall = code & 127, code >= WALL

            def local(t, carry, face=face, near=near, tiles=tiles, side=side, index=index, wall=wall):
                for q in range(2 * NV):
                    sign = -1.0 if 1 <= q <= 3 else 1.0
                    own = face[side, q * tiles + t]
                    near[side, q * tiles + t] = jnp.where(
                        wall, sign * own, take_lanes(face[1 - side, q * tiles + t], index)
                    )
                return carry

            lax.fori_loop(0, tiles, local, 0)


def surface_update(
    section, last, parity, codes, field, base, face0, face2, near0, near2, received,
    new_field, new_register, other0, other2, work,
):
    step = TIME_STEP
    flow_a, flow_b, span_a, span_b = received
    flow_odd, span_odd = parity[0], parity[1]
    for side, got in ((1 - flow_odd, flow_a), (flow_odd, flow_b)):
        code = codes[side]
        index = code & 127
        mask = (code & RECEIVED) != 0
        for g in range(4):
            shifted = index + 32 * g
            shifted = shifted & 127
            for t in range(15):
                other0[side, 15 * g + t] = jnp.where(
                    mask, take_lanes(got[t], shifted), near0[side, 15 * g + t]
                )
    for side, got in ((1 - span_odd, span_a), (span_odd, span_b)):
        code = codes[4 + side]
        index = code & 127
        mask = (code & RECEIVED) != 0
        for g in range(2):
            shifted = (index + 64 * g) & 127
            for t in range(25):
                other2[side, 25 * g + t] = jnp.where(
                    mask, take_lanes(got[t], shifted), near2[side, 25 * g + t]
                )

    def sides(own, other, tiles, t):
        result = []
        for side in range(2):
            result.append(
                (
                    [own[side, v * tiles + t] for v in range(NV)],
                    [own[side, (NV + v) * tiles + t] for v in range(NV)],
                    [other[side, v * tiles + t] for v in range(NV)],
                    [other[side, (NV + v) * tiles + t] for v in range(NV)],
                )
            )
        return result

    def span_row(chunk, carry):
        low, high = sides(face2, other2, 5, chunk)
        terms = face_terms(low, high, 2)
        for v in range(NV):
            values = [line_at(base, v, chunk, k) for k in range(6)]
            values = add_faces(values, terms, v, step)
            for k in range(6):
                put_line(work, v, chunk, k, values[k])
        return carry

    lax.fori_loop(0, 5, span_row, 0)

    def flow_row(j, carry):
        low, high = sides(face0, other0, 6, j)
        terms = face_terms(low, high, 0)
        for v in range(NV):
            rows = [v * VROWS + i * 48 + j * 8 for i in range(6)]
            values = add_faces([tile_at(work, row) for row in rows], terms, v, step)
            for i in range(6):
                updated = tile_at(field, rows[i]) + RK_B[section] * values[i]
                if last:
                    new_field[v, i, j] = updated[:6]
                    new_register[v, i, j] = values[i][:6]
                else:
                    put_tile(new_field, rows[i], updated)
                    put_tile(new_register, rows[i], values[i])
        return carry

    lax.fori_loop(0, 6, flow_row, 0)


def surface_kernel(
    section, parity, codes, field, base, face0, face2, near0, near2, ra, rb, rc, rd,
    new_field, new_register, new_face0, new_face2, flow_a, flow_b, span_a, span_b,
    other0, other2, work,
):
    surface_update(
        section, False, parity, codes, field, base, face0, face2, near0, near2, (ra, rb, rc, rd),
        new_field, new_register, other0, other2, work,
    )
    make_faces(new_field, new_face0, new_face2)
    pack_faces(parity, codes, new_face0, new_face2, flow_a, flow_b, span_a, span_b)


def last_kernel(
    section, parity, codes, field, base, face0, face2, near0, near2, ra, rb, rc, rd,
    advanced, register, other0, other2, work,
):
    surface_update(
        section, True, parity, codes, field, base, face0, face2, near0, near2, (ra, rb, rc, rd),
        advanced, register, other0, other2, work,
    )


def in_vmem(value):
    return pltpu.with_memory_space_constraint(value, pltpu.VMEM)


VMEM_SPEC = pl.BlockSpec(memory_space=pltpu.VMEM)
SMEM_SPEC = pl.BlockSpec(memory_space=pltpu.SMEM)
PARAMS = pltpu.CompilerParams(vmem_limit_bytes=32 * 1024 * 1024)


def vmem_out(shape, dtype=jnp.float32):
    return pltpu.VMEM(shape, dtype)


def face_outs():
    return [
        vmem_out(FACE0), vmem_out(FACE2), vmem_out(FLOW_PACK), vmem_out(FLOW_PACK),
        vmem_out(SPAN_PACK), vmem_out(SPAN_PACK),
    ]


def first_call(parity, conserved, lists):
    outs = [vmem_out(FIELD), vmem_out(CODES, jnp.int32)] + face_outs()
    return pl.pallas_call(
        first_kernel,
        out_shape=outs,
        in_specs=[SMEM_SPEC, VMEM_SPEC, VMEM_SPEC],
        out_specs=[VMEM_SPEC] * len(outs),
        compiler_params=PARAMS,
        name="first_faces",
    )(parity, conserved, lists)


def volume_call(section, field, register, codes, face0, face2):
    outs = [vmem_out(FIELD), vmem_out(FACE0), vmem_out(FACE2)]

    def kernel(*refs):
        if section > 0:
            volume_kernel(section, *refs)
        else:
            volume_kernel(section, refs[0], None, *refs[1:])

    args = [field, codes, face0, face2] if section == 0 else [field, register, codes, face0, face2]
    return pl.pallas_call(
        kernel,
        out_shape=outs,
        in_specs=[VMEM_SPEC] * len(args),
        out_specs=[VMEM_SPEC] * len(outs),
        scratch_shapes=[pltpu.VMEM((6 * VROWS, 128), jnp.float32)],
        compiler_params=PARAMS,
        cost_estimate=pl.CostEstimate(flops=10**7, bytes_accessed=4 * 10**6, transcendentals=0),
        name="volume",
    )(*map(in_vmem, args))


def surface_call(section, parity, *args):
    last = section == len(RK_A) - 1

    def kernel(*refs):
        (last_kernel if last else surface_kernel)(section, *refs)

    if last:
        outs = [jax.ShapeDtypeStruct((NV, 6, 6, 6, 128), jnp.float32)] * 2
    else:
        outs = [vmem_out(FIELD), vmem_out(FIELD)] + face_outs()
    return pl.pallas_call(
        kernel,
        out_shape=outs,
        in_specs=[SMEM_SPEC] + [VMEM_SPEC] * len(args),
        out_specs=[VMEM_SPEC] * len(outs),
        scratch_shapes=[
            pltpu.VMEM(FACE0, jnp.float32),
            pltpu.VMEM(FACE2, jnp.float32),
            pltpu.VMEM(FIELD, jnp.float32),
        ],
        compiler_params=PARAMS,
        name="surface",
    )(parity, *map(in_vmem, args))


def swap(value, axis, crossing):
    length = lax.axis_size(axis)
    if crossing:
        pairs = [(i, (i + 1) % length if i % 2 else (i - 1) % length) for i in range(length)]
    else:
        pairs = [(i, i ^ 1) for i in range(length)]
    return lax.ppermute(value, axis, pairs)


def body(conserved, flow_lists, span_lists, face_source):
    parity = jnp.stack([lax.axis_index("px") & 1, lax.axis_index("py") & 1]).astype(jnp.int32)
    lists = jnp.concatenate(
        [face_source, jnp.tile(flow_lists[0], (1, 4)), jnp.tile(span_lists[0], (1, 2))], axis=0
    )
    field, codes, face0, face2, *packs = first_call(parity, conserved, lists)
    register = None
    for section in range(len(RK_A)):
        flow_a, flow_b, span_a, span_b = packs
        rd = swap(span_b, "py", True)
        rc = swap(span_a, "py", False)
        rb = swap(flow_b, "px", True)
        ra = swap(flow_a, "px", False)
        base, near0, near2 = volume_call(section, field, register, codes, face0, face2)
        outs = surface_call(
            section, parity, codes, field, base, face0, face2, near0, near2, ra, rb, rc, rd
        )
        if section == len(RK_A) - 1:
            return tuple(outs)
        field, register, face0, face2, *packs = outs


def solution(mesh):
    return jax.shard_map(
        body,
        mesh=mesh,
        in_specs=(
            P(None, None, None, None, ("px", "py")),
            P(("px", "py"), None, None),
            P(("px", "py"), None, None),
            P(None, ("px", "py")),
        ),
        out_specs=(
            P(None, None, None, None, ("px", "py")),
            P(None, None, None, None, ("px", "py")),
        ),
        check_vma=False,
    )
```

```python
import math

import jax
import jax.numpy as jnp
import numpy as np
from jax import lax
from jax.experimental import pallas as pl
from jax.experimental.pallas import tpu as pltpu
from jax.sharding import PartitionSpec as P

GAMMA = 1.4
VISCOSITY = 0.02
TIME_STEP = 0.01
RK_A = (
    0.0,
    -567301805773.0 / 1357537059087.0,
    -2404267990393.0 / 2016746695238.0,
    -3550918686646.0 / 2091501179385.0,
    -1275806237668.0 / 842570457699.0,
)
RK_B = (
    1432997174477.0 / 9575080441755.0,
    5161836677717.0 / 13612068292357.0,
    1720146321549.0 / 2090206949498.0,
    3134564353537.0 / 4481467310338.0,
    2277821191437.0 / 14882151754819.0,
)


def lobatto_tables():
    inner_node = math.sqrt(1.0 / 3.0 - 2.0 * math.sqrt(7.0) / 21.0)
    outer_node = math.sqrt(1.0 / 3.0 + 2.0 * math.sqrt(7.0) / 21.0)
    points = np.array([-1.0, -outer_node, -inner_node, inner_node, outer_node, 1.0])
    legendre = (63.0 * points**5 - 70.0 * points**3 + 15.0 * points) / 8.0
    weights = 2.0 / (30.0 * legendre * legendre)
    identity = np.eye(6)
    differences = points[:, None] - points[None, :] + identity
    barycentric = 1.0 / np.prod(differences, axis=1)
    matrix = barycentric[None, :] / barycentric[:, None] / differences
    matrix = matrix * (1.0 - identity)
    matrix = matrix - identity * np.sum(matrix, axis=1)[:, None]
    return matrix, weights


DM, WEIGHTS = lobatto_tables()
DM2 = DM @ DM
LIFT = 1.0 / WEIGHTS[0]
NV = 5
VROWS = 320
FIELD = (NV * VROWS, 128)
FACE0 = (2, 60, 8, 128)
FACE2 = (2, 50, 8, 128)
FLOW_PACK = (15, 8, 128)
SPAN_PACK = (25, 8, 128)
FLOW_FAR = (16, 8, 128)
SPAN_FAR = (26, 8, 128)
CODES = (10, 8, 128)
RECEIVED = 256
WALL = 512


def tile_at(ref, row):
    return ref[pl.ds(pl.multiple_of(row, 8), 8), :]


def put_tile(ref, row, value):
    ref[pl.ds(pl.multiple_of(row, 8), 8), :] = value


def line_at(ref, var, chunk, k):
    return ref[pl.ds(var * VROWS + chunk * 64 + k, 8, stride=8), :]


def put_line(ref, var, chunk, k, value):
    ref[pl.ds(var * VROWS + chunk * 64 + k, 8, stride=8), :] = value


def take_lanes(value, index):
    return jnp.take_along_axis(value, index, axis=1, mode="promise_in_bounds")


def even_odd(values):
    even = [values[m] + values[5 - m] for m in range(3)]
    odd = [values[m] - values[5 - m] for m in range(3)]
    return even, odd


def combine(coefficients, terms):
    total = None
    for coefficient, term in zip(coefficients, terms):
        part = float(coefficient) * term
        total = part if total is None else total + part
    return total


def end_derivatives(values):
    even, odd = even_odd(values)
    first = combine([(DM[0, m] + DM[0, 5 - m]) / 2 for m in range(3)], even)
    second = combine([(DM[0, m] - DM[0, 5 - m]) / 2 for m in range(3)], odd)
    return first + second, second - first


def second_derivative(values, scale):
    even, odd = even_odd(values)
    result = [None] * 6
    for i in range(3):
        first = combine([scale * (DM2[i, m] + DM2[i, 5 - m]) / 2 for m in range(3)], even)
        second = combine([scale * (DM2[i, m] - DM2[i, 5 - m]) / 2 for m in range(3)], odd)
        result[i] = first + second
        result[5 - i] = first - second
    return result


def half_primitive(state):
    inverse = 1.0 / state[0]
    half = 0.5 * inverse
    velocity = [half * state[1], half * state[2], half * state[3]]
    kinetic = velocity[0] * state[1] + velocity[1] * state[2] + velocity[2] * state[3]
    pressure = (0.5 * (GAMMA - 1.0)) * (state[4] - kinetic)
    return [0.5 * state[0], velocity[0], velocity[1], velocity[2], pressure, half * state[4]]


def line_fluxes(nodes, direction):
    sums = [[None] * NV for _ in range(6)]

    def add(node, var, value, sign):
        old = sums[node][var]
        if old is None:
            sums[node][var] = value if sign > 0 else -value
        else:
            sums[node][var] = old + value if sign > 0 else old - value

    for i in range(6):
        for m in range(i + 1, 6):
            weight = float(2.0 * WEIGHTS[i] * DM[i, m])
            left, right = nodes[i], nodes[m]
            density, v0, v1, v2, pressure, specific = [left[n] + right[n] for n in range(6)]
            velocity = (v0, v1, v2)
            mass = (weight * density) * velocity[direction]
            scaled = weight * pressure
            flux = [mass, mass * v0, mass * v1, mass * v2, mass * specific + scaled * velocity[direction]]
            flux[1 + direction] = flux[1 + direction] + scaled
            for var in range(NV):
                add(i, var, flux[var], 1)
                add(m, var, flux[var], -1)
    return sums


def rusanov(left, right, direction):
    def parts(state):
        inverse = 1.0 / state[0]
        velocity = state[1 + direction] * inverse
        kinetic = state[1] * state[1] + state[2] * state[2] + state[3] * state[3]
        pressure = (GAMMA - 1.0) * (state[4] - 0.5 * inverse * kinetic)
        speed = jnp.abs(velocity) + jnp.sqrt(GAMMA * pressure * inverse)
        flux = [state[1 + direction], state[1] * velocity, state[2] * velocity, state[3] * velocity]
        flux.append((state[4] + pressure) * velocity)
        flux[1 + direction] = flux[1 + direction] + pressure
        return flux, speed

    left_flux, left_speed = parts(left)
    right_flux, right_speed = parts(right)
    speed = jnp.maximum(left_speed, right_speed)
    return [
        0.5 * ((left_flux[n] + right_flux[n]) - speed * (right[n] - left[n])) for n in range(NV)
    ]


def face_terms(low, high, direction):
    low_flux = rusanov(low[2], low[0], direction)
    high_flux = rusanov(high[0], high[2], direction)
    visc = 0.5 * VISCOSITY * LIFT
    end_low, end_high, jump_low, jump_high = [], [], [], []
    for n in range(NV):
        end_low.append(LIFT * low_flux[n] - visc * (low[3][n] - low[1][n]))
        end_high.append(visc * (high[3][n] - high[1][n]) - LIFT * high_flux[n])
        jump_low.append(visc * (low[2][n] - low[0][n]))
        jump_high.append(visc * (high[2][n] - high[0][n]))
    return end_low, end_high, jump_low, jump_high


def add_faces(values, terms, var, scale):
    end_low, end_high, jump_low, jump_high = terms
    result = []
    for i in range(6):
        value = values[i] + float(scale * DM[i, 5]) * jump_high[var] - float(scale * DM[i, 0]) * jump_low[var]
        if i == 0:
            value = value + scale * end_low[var]
        if i == 5:
            value = value + scale * end_high[var]
        result.append(value)
    return result


def make_faces(field, face0, face2):
    faces_flow(field, face0)
    faces_span(field, face2)


def faces_flow(field, face0):
    def flow_row(j, carry):
        for v in range(NV):
            values = [tile_at(field, v * VROWS + i * 48 + j * 8) for i in range(6)]
            first, last = end_derivatives(values)
            face0[0, v * 6 + j] = values[0]
            face0[1, v * 6 + j] = values[5]
            face0[0, (NV + v) * 6 + j] = first
            face0[1, (NV + v) * 6 + j] = last
        return carry

    lax.fori_loop(0, 6, flow_row, 0)


def faces_span(field, face2):
    def span_row(chunk, carry):
        for v in range(NV):
            values = [line_at(field, v, chunk, k) for k in range(6)]
            first, last = end_derivatives(values)
            face2[0, v * 5 + chunk] = values[0]
            face2[1, v * 5 + chunk] = values[5]
            face2[0, (NV + v) * 5 + chunk] = first
            face2[1, (NV + v) * 5 + chunk] = last
        return carry

    lax.fori_loop(0, 5, span_row, 0)


def pack_faces(codes, face0, face2, flow_a, flow_b, span_a, span_b):
    lane = lax.broadcasted_iota(jnp.int32, (8, 128), 1)
    flow_odd, span_odd = lax.axis_index("px") & 1, lax.axis_index("py") & 1
    for side, out in ((1 - span_odd, span_a), (span_odd, span_b)):
        index = codes[8 + side]
        for t in range(25):
            out[t] = jnp.where(
                lane >= 64, take_lanes(face2[side, 25 + t], index), take_lanes(face2[side, t], index)
            )
    for side, out in ((1 - flow_odd, flow_a), (flow_odd, flow_b)):
        index = codes[6 + side]
        for t in range(15):
            packed = take_lanes(face0[side, t], index)
            for g in range(1, 4):
                packed = jnp.where(lane >= 32 * g, take_lanes(face0[side, 15 * g + t], index), packed)
            out[t] = packed


def first_kernel(
    conserved, flow_lists, span_lists, face_source, field, codes, face0, face2,
    flow_a, flow_b, span_a, span_b, state, flow_rows, span_rows, columns, list_sems, state_sems,
):
    copies = [
        pltpu.make_async_copy(source, target, list_sems.at[n])
        for n, (source, target) in enumerate(
            ((flow_lists, flow_rows), (span_lists, span_rows), (face_source, columns))
        )
    ]
    copies += [pltpu.make_async_copy(conserved.at[v], state.at[v], state_sems.at[v]) for v in range(NV)]
    for copy in copies:
        copy.start()
    for copy in copies[:3]:
        copy.wait()
    for side in range(6):
        column = columns[pl.ds(side, 1), :]
        mask = 31 if side < 2 else 63
        offset = 768 if side < 2 else 832
        code = jnp.where(
            column < 768,
            column & 127,
            jnp.where(column < 960, ((column - offset) & mask) + RECEIVED, WALL),
        )
        codes[side] = jnp.broadcast_to(code, (8, 128))
    for side in range(2):
        flow_row = jnp.concatenate([flow_rows[0, pl.ds(side, 1), :]] * 4, axis=1)
        span_row = jnp.concatenate([span_rows[0, pl.ds(side, 1), :]] * 2, axis=1)
        codes[6 + side] = jnp.broadcast_to(flow_row, (8, 128))
        codes[8 + side] = jnp.broadcast_to(span_row, (8, 128))
    for v in range(NV):
        copies[3 + v].wait()
        for i in range(6):
            for j in range(6):
                field[pl.ds(v * VROWS + i * 48 + j * 8, 6), :] = state[v, i, j]
    make_faces(field, face0, face2)
    pack_faces(codes, face0, face2, flow_a, flow_b, span_a, span_b)


def volume_kernel(
    section, field, register, codes, face0, face2, base, near0, near2, prims, face1, near1
):
    volume_primitives(field, prims)
    wall_faces(field, face1)
    volume_flow(section, field, register, codes, base, prims, face1, near1)
    volume_wall(field, codes, base, prims, face1, near1, face0, near0)
    volume_span(field, codes, base, prims, face2, near2)


def take_local(codes, first_side, face, near, tiles, t):
    for side in range(2):
        index = codes[first_side + side] & 127
        for q in range(2 * NV):
            near[side, q * tiles + t] = take_lanes(face[1 - side, q * tiles + t], index)


def volume_primitives(field, prims):
    def primitives(n, carry):
        for u in range(4):
            row = (n * 4 + u) * 8
            values = half_primitive([tile_at(field, v * VROWS + row) for v in range(NV)])
            for q in range(6):
                put_tile(prims, q * VROWS + row, values[q])
        return carry

    lax.fori_loop(0, 9, primitives, 0)


def volume_flow(section, field, register, codes, base, prims, face1, near1):
    step = TIME_STEP

    def flow_row(j, carry):
        row = j * 8
        nodes = [[tile_at(prims, q * VROWS + i * 48 + row) for q in range(6)] for i in range(6)]
        sums = line_fluxes(nodes, 0)
        for v in range(NV):
            line = [tile_at(field, v * VROWS + i * 48 + row) for i in range(6)]
            second = second_derivative(line, step * VISCOSITY)
            for i in range(6):
                value = second[i] - float(step / WEIGHTS[i]) * sums[i][v]
                if section > 0:
                    value = value + RK_A[section] * tile_at(register, v * VROWS + i * 48 + row)
                put_tile(base, v * VROWS + i * 48 + row, value)
        take_local(codes, 2, face1, near1, 6, j)
        return carry

    lax.fori_loop(0, 6, flow_row, 0)


def wall_faces(field, face1):
    def wall_row(i, carry):
        for v in range(NV):
            values = [tile_at(field, v * VROWS + i * 48 + j * 8) for j in range(6)]
            first, last = end_derivatives(values)
            face1[0, v * 6 + i] = values[0]
            face1[1, v * 6 + i] = values[5]
            face1[0, (NV + v) * 6 + i] = first
            face1[1, (NV + v) * 6 + i] = last
        return carry

    lax.fori_loop(0, 6, wall_row, 0)


def volume_wall(field, codes, base, prims, face1, near1, face0, near0):
    step = TIME_STEP

    def wall_row(i, carry):
        row = i * 48
        nodes = [[tile_at(prims, q * VROWS + row + j * 8) for q in range(6)] for j in range(6)]
        sums = line_fluxes(nodes, 1)
        low, high = sides(codes, 2, face1, near1, 6, i)
        terms = face_terms(low, high, 1)
        for v in range(NV):
            line = [tile_at(field, v * VROWS + row + j * 8) for j in range(6)]
            second = second_derivative(line, step * VISCOSITY)
            values = [second[j] - float(step / WEIGHTS[j]) * sums[j][v] for j in range(6)]
            values = add_faces(values, terms, v, step)
            for j in range(6):
                where = v * VROWS + row + j * 8
                put_tile(base, where, tile_at(base, where) + values[j])
        take_local(codes, 0, face0, near0, 6, i)
        return carry

    lax.fori_loop(0, 6, wall_row, 0)


def volume_span(field, codes, base, prims, face2, near2):
    step = TIME_STEP

    def span_row(chunk, carry):
        nodes = [[line_at(prims, q, chunk, k) for q in range(6)] for k in range(6)]
        sums = line_fluxes(nodes, 2)
        for v in range(NV):
            line = [line_at(field, v, chunk, k) for k in range(6)]
            second = second_derivative(line, step * VISCOSITY)
            for k in range(6):
                value = second[k] - float(step / WEIGHTS[k]) * sums[k][v]
                put_line(base, v, chunk, k, line_at(base, v, chunk, k) + value)
        take_local(codes, 4, face2, near2, 5, chunk)
        return carry

    lax.fori_loop(0, 5, span_row, 0)


def surface_update(
    section, last, codes, field, base, face0, face2, near0, near2, received,
    new_field, new_register, got0, got2, work,
):
    flow_a, flow_b, span_a, span_b = received
    flow_odd, span_odd = lax.axis_index("px") & 1, lax.axis_index("py") & 1
    got2[1 - span_odd] = span_a[...]
    got2[span_odd] = span_b[pl.ds(0, 25)]
    got0[1 - flow_odd] = flow_a[...]
    got0[flow_odd] = flow_b[pl.ds(0, 15)]
    surface_span(codes, base, face2, near2, got2, work)
    surface_flow(section, last, codes, field, face0, near0, got0, new_field, new_register, work)


def sides(codes, first_side, own, near, tiles, t, got=None, groups=1):
    result = []
    for side in range(2):
        code = codes[first_side + side]
        wall = code >= WALL
        received = (code & RECEIVED) != 0
        own_values, other_values = [], []
        for q in range(2 * NV):
            row = q * tiles + t
            own_value = own[side, row]
            other_value = near[side, row]
            if got is not None:
                share = 2 * NV * tiles // groups
                index = (code + (128 // groups) * (row // share)) & 127
                other_value = jnp.where(received, take_lanes(got[side, row % share], index), other_value)
            mirrored = -own_value if 1 <= q <= 3 else own_value
            own_values.append(own_value)
            other_values.append(jnp.where(wall, mirrored, other_value))
        result.append((own_values[:NV], own_values[NV:], other_values[:NV], other_values[NV:]))
    return result


def surface_span(codes, base, face2, near2, got2, work):
    step = TIME_STEP

    def span_row(chunk, carry):
        low, high = sides(codes, 4, face2, near2, 5, chunk, got2, 2)
        terms = face_terms(low, high, 2)
        for v in range(NV):
            values = [line_at(base, v, chunk, k) for k in range(6)]
            values = add_faces(values, terms, v, step)
            for k in range(6):
                put_line(work, v, chunk, k, values[k])
        return carry

    for chunk in range(5):
        span_row(chunk, 0)


def surface_flow(section, last, codes, field, face0, near0, got0, new_field, new_register, work):
    step = TIME_STEP

    def flow_row(j, carry):
        low, high = sides(codes, 0, face0, near0, 6, j, got0, 4)
        terms = face_terms(low, high, 0)
        for v in range(NV):
            rows = [v * VROWS + i * 48 + j * 8 for i in range(6)]
            values = add_faces([tile_at(work, row) for row in rows], terms, v, step)
            for i in range(6):
                updated = tile_at(field, rows[i]) + RK_B[section] * values[i]
                if last:
                    new_field[v, i, j] = updated[:6]
                    new_register[v, i, j] = values[i][:6]
                else:
                    put_tile(new_field, rows[i], updated)
                    put_tile(new_register, rows[i], values[i])
        return carry

    for j in range(6):
        flow_row(j, 0)


def surface_kernel(
    section, codes, field, base, face0, face2, near0, near2, ra, rb, rc, rd,
    new_field, new_register, new_face0, new_face2, flow_a, flow_b, span_a, span_b,
    got0, got2, work,
):
    surface_update(
        section, False, codes, field, base, face0, face2, near0, near2, (ra, rb, rc, rd),
        new_field, new_register, got0, got2, work,
    )
    make_faces(new_field, new_face0, new_face2)
    pack_faces(codes, new_face0, new_face2, flow_a, flow_b, span_a, span_b)


def last_kernel(
    section, codes, field, base, face0, face2, near0, near2, ra, rb, rc, rd,
    advanced, register, got0, got2, work,
):
    surface_update(
        section, True, codes, field, base, face0, face2, near0, near2, (ra, rb, rc, rd),
        advanced, register, got0, got2, work,
    )


def in_vmem(value):
    return pltpu.with_memory_space_constraint(value, pltpu.VMEM)


VMEM_SPEC = pl.BlockSpec(memory_space=pltpu.VMEM)
PARAMS = pltpu.CompilerParams(vmem_limit_bytes=32 * 1024 * 1024)


def vmem_out(shape, dtype=jnp.float32):
    return pltpu.VMEM(shape, dtype)


def face_outs():
    return [
        vmem_out(FACE0), vmem_out(FACE2), vmem_out(FLOW_PACK), vmem_out(FLOW_FAR),
        vmem_out(SPAN_PACK), vmem_out(SPAN_FAR),
    ]


def first_call(*args):
    outs = [vmem_out(FIELD), vmem_out(CODES, jnp.int32)] + face_outs()
    return pl.pallas_call(
        first_kernel,
        out_shape=outs,
        in_specs=[pl.BlockSpec(memory_space=pltpu.HBM)] * len(args),
        out_specs=[VMEM_SPEC] * len(outs),
        scratch_shapes=[
            pltpu.VMEM((NV, 6, 6, 6, 128), jnp.float32),
            pltpu.VMEM((1, 2, 32), jnp.int32),
            pltpu.VMEM((1, 2, 64), jnp.int32),
            pltpu.VMEM((6, 128), jnp.int32),
            pltpu.SemaphoreType.DMA((3,)),
            pltpu.SemaphoreType.DMA((NV,)),
        ],
        compiler_params=PARAMS,
        name="first_faces",
    )(*[pltpu.with_memory_space_constraint(value, pltpu.HBM) for value in args])


def volume_call(section, field, register, codes, face0, face2):
    def kernel(*refs):
        if section > 0:
            volume_kernel(section, *refs)
        else:
            volume_kernel(section, refs[0], None, *refs[1:])

    args = [field, codes, face0, face2] if section == 0 else [field, register, codes, face0, face2]
    outs = [vmem_out(FIELD), vmem_out(FACE0), vmem_out(FACE2)]
    return pl.pallas_call(
        kernel,
        out_shape=outs,
        in_specs=[VMEM_SPEC] * len(args),
        out_specs=[VMEM_SPEC] * len(outs),
        scratch_shapes=[
            pltpu.VMEM((6 * VROWS, 128), jnp.float32),
            pltpu.VMEM(FACE0, jnp.float32),
            pltpu.VMEM(FACE0, jnp.float32),
        ],
        compiler_params=PARAMS,
        cost_estimate=pl.CostEstimate(flops=10**7, bytes_accessed=4 * 10**6, transcendentals=0),
        name="volume",
    )(*map(in_vmem, args))


def surface_call(section, *args):
    last = section == len(RK_A) - 1

    def kernel(*refs):
        (last_kernel if last else surface_kernel)(section, *refs)

    if last:
        outs = [jax.ShapeDtypeStruct((NV, 6, 6, 6, 128), jnp.float32)] * 2
    else:
        outs = [vmem_out(FIELD), vmem_out(FIELD)] + face_outs()
    return pl.pallas_call(
        kernel,
        out_shape=outs,
        in_specs=[VMEM_SPEC] * len(args),
        out_specs=[VMEM_SPEC] * len(outs),
        scratch_shapes=[
            pltpu.VMEM((2,) + FLOW_PACK, jnp.float32),
            pltpu.VMEM((2,) + SPAN_PACK, jnp.float32),
            pltpu.VMEM(FIELD, jnp.float32),
        ],
        compiler_params=PARAMS,
        name="surface",
    )(*map(in_vmem, args))


def swap(value, axis, crossing):
    length = lax.axis_size(axis)
    if crossing:
        pairs = [(i, (i + 1) % length if i % 2 else (i - 1) % length) for i in range(length)]
    else:
        pairs = [(i, i ^ 1) for i in range(length)]
    return lax.ppermute(value, axis, pairs)


def body(conserved, flow_lists, span_lists, face_source):
    field, codes, *faces = first_call(conserved, flow_lists, span_lists, face_source)
    register = None
    for section in range(len(RK_A)):
        face0, face2, flow_a, flow_b, span_a, span_b = faces
        rd = swap(span_b, "py", True)
        rc = swap(span_a, "py", False)
        rb = swap(flow_b, "px", True)
        ra = swap(flow_a, "px", False)
        base, near0, near2 = volume_call(section, field, register, codes, face0, face2)
        outs = surface_call(
            section, codes, field, base, face0, face2, near0, near2, ra, rb, rc, rd
        )
        if section == len(RK_A) - 1:
            return tuple(outs)
        field, register, *faces = outs


def solution(mesh):
    return jax.shard_map(
        body,
        mesh=mesh,
        in_specs=(
            P(None, None, None, None, ("px", "py")),
            P(("px", "py"), None, None),
            P(("px", "py"), None, None),
            P(None, ("px", "py")),
        ),
        out_specs=(
            P(None, None, None, None, ("px", "py")),
            P(None, None, None, None, ("px", "py")),
        ),
        check_vma=False,
    )
```

```python
import math

import jax
import jax.numpy as jnp
import numpy as np
from jax import lax
from jax.experimental import pallas as pl
from jax.experimental.pallas import tpu as pltpu
from jax.sharding import PartitionSpec as P

GAMMA = 1.4
VISCOSITY = 0.02
TIME_STEP = 0.01
RK_A = (
    0.0,
    -567301805773.0 / 1357537059087.0,
    -2404267990393.0 / 2016746695238.0,
    -3550918686646.0 / 2091501179385.0,
    -1275806237668.0 / 842570457699.0,
)
RK_B = (
    1432997174477.0 / 9575080441755.0,
    5161836677717.0 / 13612068292357.0,
    1720146321549.0 / 2090206949498.0,
    3134564353537.0 / 4481467310338.0,
    2277821191437.0 / 14882151754819.0,
)


def lobatto_tables():
    inner_node = math.sqrt(1.0 / 3.0 - 2.0 * math.sqrt(7.0) / 21.0)
    outer_node = math.sqrt(1.0 / 3.0 + 2.0 * math.sqrt(7.0) / 21.0)
    points = np.array([-1.0, -outer_node, -inner_node, inner_node, outer_node, 1.0])
    legendre = (63.0 * points**5 - 70.0 * points**3 + 15.0 * points) / 8.0
    weights = 2.0 / (30.0 * legendre * legendre)
    identity = np.eye(6)
    differences = points[:, None] - points[None, :] + identity
    barycentric = 1.0 / np.prod(differences, axis=1)
    matrix = barycentric[None, :] / barycentric[:, None] / differences
    matrix = matrix * (1.0 - identity)
    matrix = matrix - identity * np.sum(matrix, axis=1)[:, None]
    return matrix, weights


DM, WEIGHTS = lobatto_tables()
DM2 = DM @ DM
LIFT = 1.0 / WEIGHTS[0]
NV = 5
VROWS = 320
FIELD = (NV * VROWS, 128)
FACE0 = (2, 60, 8, 128)
FACE2 = (2, 50, 8, 128)
FLOW_PACK = (15, 8, 128)
SPAN_PACK = (25, 8, 128)
FLOW_FAR = (16, 8, 128)
SPAN_FAR = (26, 8, 128)
CODES = (10, 8, 128)
RECEIVED = 256
WALL = 512


def tile_at(ref, row):
    return ref[pl.ds(pl.multiple_of(row, 8), 8), :]


def put_tile(ref, row, value):
    ref[pl.ds(pl.multiple_of(row, 8), 8), :] = value


def line_at(ref, var, chunk, k):
    return ref[pl.ds(var * VROWS + chunk * 64 + k, 8, stride=8), :]


def put_line(ref, var, chunk, k, value):
    ref[pl.ds(var * VROWS + chunk * 64 + k, 8, stride=8), :] = value


def rows_loop(count, unroll, row):
    def step(n, carry):
        for u in range(unroll):
            row(n * unroll + u, carry)
        return carry

    if unroll == count:
        step(0, 0)
    else:
        lax.fori_loop(0, count // unroll, step, 0)


def take_lanes(value, index):
    return jnp.take_along_axis(value, index, axis=1, mode="promise_in_bounds")


def even_odd(values):
    even = [values[m] + values[5 - m] for m in range(3)]
    odd = [values[m] - values[5 - m] for m in range(3)]
    return even, odd


def combine(coefficients, terms):
    total = None
    for coefficient, term in zip(coefficients, terms):
        part = float(coefficient) * term
        total = part if total is None else total + part
    return total


def end_derivatives(values):
    even, odd = even_odd(values)
    first = combine([(DM[0, m] + DM[0, 5 - m]) / 2 for m in range(3)], even)
    second = combine([(DM[0, m] - DM[0, 5 - m]) / 2 for m in range(3)], odd)
    return first + second, second - first


def jump_parts(low, high):
    total, difference = high + low, high - low
    even = [float((DM[i, 5] + DM[5 - i, 5]) / 2) * total for i in range(3)]
    odd = [float((DM[i, 5] - DM[5 - i, 5]) / 2) * difference for i in range(3)]
    return even, odd


def second_derivative(values, scale, jumps=None):
    even, odd = even_odd(values)
    result = [None] * 6
    for i in range(3):
        first = combine([scale * (DM2[i, m] + DM2[i, 5 - m]) / 2 for m in range(3)], even)
        second = combine([scale * (DM2[i, m] - DM2[i, 5 - m]) / 2 for m in range(3)], odd)
        if jumps is not None:
            first, second = first + jumps[0][i], second + jumps[1][i]
        result[i] = first + second
        result[5 - i] = first - second
    return result


def half_primitive(state):
    inverse = 1.0 / state[0]
    half = 0.5 * inverse
    velocity = [half * state[1], half * state[2], half * state[3]]
    kinetic = velocity[0] * state[1] + velocity[1] * state[2] + velocity[2] * state[3]
    pressure = (0.5 * (GAMMA - 1.0)) * (state[4] - kinetic)
    return [0.5 * state[0], velocity[0], velocity[1], velocity[2], pressure, half * state[4]]


def line_fluxes(nodes, direction):
    sums = [[None] * NV for _ in range(6)]

    def add(node, var, value, sign):
        old = sums[node][var]
        if old is None:
            sums[node][var] = value if sign > 0 else -value
        else:
            sums[node][var] = old + value if sign > 0 else old - value

    for i in range(6):
        for m in range(i + 1, 6):
            weight = float(2.0 * WEIGHTS[i] * DM[i, m])
            left, right = nodes[i], nodes[m]
            density, v0, v1, v2, pressure, specific = [left[n] + right[n] for n in range(6)]
            velocity = (v0, v1, v2)
            mass = (weight * density) * velocity[direction]
            scaled = weight * pressure
            flux = [mass, mass * v0, mass * v1, mass * v2, mass * specific + scaled * velocity[direction]]
            flux[1 + direction] = flux[1 + direction] + scaled
            for var in range(NV):
                add(i, var, flux[var], 1)
                add(m, var, flux[var], -1)
    return sums


def rusanov(left, right, direction, scale):
    def parts(state):
        inverse = 1.0 / state[0]
        velocity = state[1 + direction] * inverse
        kinetic = state[1] * state[1] + state[2] * state[2] + state[3] * state[3]
        pressure = (GAMMA - 1.0) * (state[4] - 0.5 * inverse * kinetic)
        speed = jnp.abs(velocity) + jnp.sqrt(GAMMA * pressure * inverse)
        flux = [state[1 + direction], state[1] * velocity, state[2] * velocity, state[3] * velocity]
        flux.append((state[4] + pressure) * velocity)
        flux[1 + direction] = flux[1 + direction] + pressure
        return flux, speed

    left_flux, left_speed = parts(left)
    right_flux, right_speed = parts(right)
    speed = jnp.maximum(left_speed, right_speed)
    return [
        (0.5 * scale) * ((left_flux[n] + right_flux[n]) - speed * (right[n] - left[n]))
        for n in range(NV)
    ]


def face_terms(low, high, direction):
    low_flux = rusanov(low[2], low[0], direction, TIME_STEP * LIFT)
    high_flux = rusanov(high[0], high[2], direction, TIME_STEP * LIFT)
    visc = TIME_STEP * 0.5 * VISCOSITY * LIFT
    ends_low, ends_high, jumps = [], [], []
    for n in range(NV):
        ends_low.append(low_flux[n] - visc * (low[3][n] - low[1][n]))
        ends_high.append(visc * (high[3][n] - high[1][n]) - high_flux[n])
        jumps.append(jump_parts(visc * (low[2][n] - low[0][n]), visc * (high[2][n] - high[0][n])))
    return ends_low, ends_high, jumps


def add_faces(values, terms, var):
    ends_low, ends_high, jumps = terms
    even, odd = jumps[var]
    result = [None] * 6
    for i in range(3):
        result[i] = values[i] + (even[i] + odd[i])
        result[5 - i] = values[5 - i] + (even[i] - odd[i])
    result[0] = result[0] + ends_low[var]
    result[5] = result[5] + ends_high[var]
    return result


def make_faces(field, face0, face2):
    faces_flow(field, face0)
    faces_span(field, face2)


def faces_flow(field, face0):
    def flow_row(j, carry):
        for v in range(NV):
            values = [tile_at(field, v * VROWS + i * 48 + j * 8) for i in range(6)]
            first, last = end_derivatives(values)
            face0[0, v * 6 + j] = values[0]
            face0[1, v * 6 + j] = values[5]
            face0[0, (NV + v) * 6 + j] = first
            face0[1, (NV + v) * 6 + j] = last
        return carry

    rows_loop(6, 6, flow_row)


def faces_span(field, face2):
    def span_row(chunk, carry):
        for v in range(NV):
            values = [line_at(field, v, chunk, k) for k in range(6)]
            first, last = end_derivatives(values)
            face2[0, v * 5 + chunk] = values[0]
            face2[1, v * 5 + chunk] = values[5]
            face2[0, (NV + v) * 5 + chunk] = first
            face2[1, (NV + v) * 5 + chunk] = last
        return carry

    rows_loop(5, 5, span_row)


def pack_faces(codes, face0, face2, flow_a, flow_b, span_a, span_b):
    lane = lax.broadcasted_iota(jnp.int32, (8, 128), 1)
    flow_odd, span_odd = lax.axis_index("px") & 1, lax.axis_index("py") & 1
    for side, out in ((1 - span_odd, span_a), (span_odd, span_b)):
        index = codes[8 + side]
        for t in range(25):
            out[t] = jnp.where(
                lane >= 64, take_lanes(face2[side, 25 + t], index), take_lanes(face2[side, t], index)
            )
    for side, out in ((1 - flow_odd, flow_a), (flow_odd, flow_b)):
        index = codes[6 + side]
        for t in range(15):
            packed = take_lanes(face0[side, t], index)
            for g in range(1, 4):
                packed = jnp.where(lane >= 32 * g, take_lanes(face0[side, 15 * g + t], index), packed)
            out[t] = packed


def first_kernel(
    conserved, flow_lists, span_lists, face_source, field, codes, face0, face2,
    flow_a, flow_b, span_a, span_b, state, flow_rows, span_rows, columns, list_sems, state_sems,
):
    copies = [
        pltpu.make_async_copy(source, target, list_sems.at[n])
        for n, (source, target) in enumerate(
            ((flow_lists, flow_rows), (span_lists, span_rows), (face_source, columns))
        )
    ]
    copies += [pltpu.make_async_copy(conserved.at[v], state.at[v], state_sems.at[v]) for v in range(NV)]
    for copy in copies:
        copy.start()
    for copy in copies[:3]:
        copy.wait()
    for side in range(6):
        column = columns[pl.ds(side, 1), :]
        mask = 31 if side < 2 else 63
        offset = 768 if side < 2 else 832
        code = jnp.where(
            column < 768,
            column & 127,
            jnp.where(column < 960, ((column - offset) & mask) + RECEIVED, WALL),
        )
        codes[side] = jnp.broadcast_to(code, (8, 128))
    for side in range(2):
        flow_row = jnp.concatenate([flow_rows[0, pl.ds(side, 1), :]] * 4, axis=1)
        span_row = jnp.concatenate([span_rows[0, pl.ds(side, 1), :]] * 2, axis=1)
        codes[6 + side] = jnp.broadcast_to(flow_row, (8, 128))
        codes[8 + side] = jnp.broadcast_to(span_row, (8, 128))
    for v in range(NV):
        copies[3 + v].wait()
        for i in range(6):
            for j in range(6):
                field[pl.ds(v * VROWS + i * 48 + j * 8, 6), :] = state[v, i, j]
    make_faces(field, face0, face2)
    pack_faces(codes, face0, face2, flow_a, flow_b, span_a, span_b)


def volume_kernel(
    section, field, register, codes, face0, face2, base, near0, near2, prims, face1, near1
):
    volume_primitives(field, prims)
    wall_faces(field, face1)
    volume_flow(section, field, register, codes, base, prims, face1, near1)
    volume_wall(field, codes, base, prims, face1, near1, face0, near0)
    volume_span(field, codes, base, prims, face2, near2)


def take_local(codes, first_side, face, near, tiles, t):
    for side in range(2):
        index = codes[first_side + side] & 127
        for q in range(2 * NV):
            near[side, q * tiles + t] = take_lanes(face[1 - side, q * tiles + t], index)


def volume_primitives(field, prims):
    def primitives(n, carry):
        for u in range(4):
            row = (n * 4 + u) * 8
            values = half_primitive([tile_at(field, v * VROWS + row) for v in range(NV)])
            for q in range(6):
                put_tile(prims, q * VROWS + row, values[q])
        return carry

    rows_loop(9, 9, primitives)


def volume_flow(section, field, register, codes, base, prims, face1, near1):
    step = TIME_STEP

    def flow_row(j, carry):
        row = j * 8
        nodes = [[tile_at(prims, q * VROWS + i * 48 + row) for q in range(6)] for i in range(6)]
        sums = line_fluxes(nodes, 0)
        for v in range(NV):
            line = [tile_at(field, v * VROWS + i * 48 + row) for i in range(6)]
            second = second_derivative(line, step * VISCOSITY)
            for i in range(6):
                value = second[i] - float(step / WEIGHTS[i]) * sums[i][v]
                if section > 0:
                    value = value + RK_A[section] * tile_at(register, v * VROWS + i * 48 + row)
                put_tile(base, v * VROWS + i * 48 + row, value)
        take_local(codes, 2, face1, near1, 6, j)
        return carry

    lax.fori_loop(0, 6, flow_row, 0)


def wall_faces(field, face1):
    def wall_row(i, carry):
        for v in range(NV):
            values = [tile_at(field, v * VROWS + i * 48 + j * 8) for j in range(6)]
            first, last = end_derivatives(values)
            face1[0, v * 6 + i] = values[0]
            face1[1, v * 6 + i] = values[5]
            face1[0, (NV + v) * 6 + i] = first
            face1[1, (NV + v) * 6 + i] = last
        return carry

    rows_loop(6, 6, wall_row)


def volume_wall(field, codes, base, prims, face1, near1, face0, near0):
    step = TIME_STEP

    def wall_row(i, carry):
        row = i * 48
        nodes = [[tile_at(prims, q * VROWS + row + j * 8) for q in range(6)] for j in range(6)]
        sums = line_fluxes(nodes, 1)
        low, high = sides(codes, 2, face1, near1, 6, i)
        terms = face_terms(low, high, 1)
        for v in range(NV):
            line = [tile_at(field, v * VROWS + row + j * 8) for j in range(6)]
            second = second_derivative(line, step * VISCOSITY, terms[2][v])
            values = [second[j] - float(step / WEIGHTS[j]) * sums[j][v] for j in range(6)]
            values[0] = values[0] + terms[0][v]
            values[5] = values[5] + terms[1][v]
            for j in range(6):
                where = v * VROWS + row + j * 8
                put_tile(base, where, tile_at(base, where) + values[j])
        take_local(codes, 0, face0, near0, 6, i)
        return carry

    lax.fori_loop(0, 6, wall_row, 0)


def volume_span(field, codes, base, prims, face2, near2):
    step = TIME_STEP

    def span_row(chunk, carry):
        nodes = [[line_at(prims, q, chunk, k) for q in range(6)] for k in range(6)]
        sums = line_fluxes(nodes, 2)
        for v in range(NV):
            line = [line_at(field, v, chunk, k) for k in range(6)]
            second = second_derivative(line, step * VISCOSITY)
            for k in range(6):
                value = second[k] - float(step / WEIGHTS[k]) * sums[k][v]
                put_line(base, v, chunk, k, line_at(base, v, chunk, k) + value)
        take_local(codes, 4, face2, near2, 5, chunk)
        return carry

    lax.fori_loop(0, 5, span_row, 0)


def surface_update(
    section, last, codes, field, base, face0, face2, near0, near2, received,
    new_field, new_register, got0, got2, work, *staging,
):
    flow_a, flow_b, span_a, span_b = received
    flow_odd, span_odd = lax.axis_index("px") & 1, lax.axis_index("py") & 1
    got2[1 - span_odd] = span_a[...]
    got2[span_odd] = span_b[pl.ds(0, 25)]
    got0[1 - flow_odd] = flow_a[...]
    got0[flow_odd] = flow_b[pl.ds(0, 15)]
    surface_span(codes, base, face2, near2, got2, work)
    surface_flow(
        section, last, codes, field, face0, near0, got0, new_field, new_register, work, *staging
    )


def sides(codes, first_side, own, near, tiles, t, got=None, groups=1):
    result = []
    for side in range(2):
        code = codes[first_side + side]
        wall = code >= WALL
        received = (code & RECEIVED) != 0
        own_values, other_values = [], []
        for q in range(2 * NV):
            row = q * tiles + t
            own_value = own[side, row]
            other_value = near[side, row]
            if got is not None:
                share = 2 * NV * tiles // groups
                index = (code + (128 // groups) * (row // share)) & 127
                other_value = jnp.where(received, take_lanes(got[side, row % share], index), other_value)
            mirrored = -own_value if 1 <= q <= 3 else own_value
            own_values.append(own_value)
            other_values.append(jnp.where(wall, mirrored, other_value))
        result.append((own_values[:NV], own_values[NV:], other_values[:NV], other_values[NV:]))
    return result


def surface_span(codes, base, face2, near2, got2, work):
    def span_row(chunk, carry):
        low, high = sides(codes, 4, face2, near2, 5, chunk, got2, 2)
        terms = face_terms(low, high, 2)
        for v in range(NV):
            values = [line_at(base, v, chunk, k) for k in range(6)]
            values = add_faces(values, terms, v)
            for k in range(6):
                put_line(work, v, chunk, k, values[k])
        return carry

    rows_loop(5, 5, span_row)


def surface_flow(
    section, last, codes, field, face0, near0, got0, new_field, new_register, work,
    out_state=None, out_register=None, sems=None,
):
    copies = []

    def flow_row(j, carry):
        low, high = sides(codes, 0, face0, near0, 6, j, got0, 4)
        terms = face_terms(low, high, 0)
        for v in range(NV):
            rows = [v * VROWS + i * 48 + j * 8 for i in range(6)]
            values = add_faces([tile_at(work, row) for row in rows], terms, v)
            for i in range(6):
                updated = tile_at(field, rows[i]) + RK_B[section] * values[i]
                if last:
                    out_state[v, i, j] = updated[:6]
                    out_register[v, i, j] = values[i][:6]
                else:
                    put_tile(new_field, rows[i], updated)
                    put_tile(new_register, rows[i], values[i])
        if last:
            for n, (source, target) in enumerate(((out_state, new_field), (out_register, new_register))):
                copy = pltpu.make_async_copy(source.at[:, :, j], target.at[:, :, j], sems.at[n, j])
                copy.start()
                copies.append(copy)
        return carry

    rows_loop(6, 6, flow_row)
    for copy in copies:
        copy.wait()


def surface_kernel(
    section, codes, field, base, face0, face2, near0, near2, ra, rb, rc, rd,
    new_field, new_register, new_face0, new_face2, flow_a, flow_b, span_a, span_b,
    got0, got2, work,
):
    surface_update(
        section, False, codes, field, base, face0, face2, near0, near2, (ra, rb, rc, rd),
        new_field, new_register, got0, got2, work,
    )
    make_faces(new_field, new_face0, new_face2)
    pack_faces(codes, new_face0, new_face2, flow_a, flow_b, span_a, span_b)


def last_kernel(
    section, codes, field, base, face0, face2, near0, near2, ra, rb, rc, rd,
    advanced, register, got0, got2, work, *staging,
):
    surface_update(
        section, True, codes, field, base, face0, face2, near0, near2, (ra, rb, rc, rd),
        advanced, register, got0, got2, work, *staging,
    )


def in_vmem(value):
    return pltpu.with_memory_space_constraint(value, pltpu.VMEM)


VMEM_SPEC = pl.BlockSpec(memory_space=pltpu.VMEM)
PARAMS = pltpu.CompilerParams(vmem_limit_bytes=32 * 1024 * 1024)


def vmem_out(shape, dtype=jnp.float32):
    return pltpu.VMEM(shape, dtype)


def face_outs():
    return [
        vmem_out(FACE0), vmem_out(FACE2), vmem_out(FLOW_PACK), vmem_out(FLOW_FAR),
        vmem_out(SPAN_PACK), vmem_out(SPAN_FAR),
    ]


def first_call(*args):
    outs = [vmem_out(FIELD), vmem_out(CODES, jnp.int32)] + face_outs()
    return pl.pallas_call(
        first_kernel,
        out_shape=outs,
        in_specs=[pl.BlockSpec(memory_space=pltpu.HBM)] * len(args),
        out_specs=[VMEM_SPEC] * len(outs),
        scratch_shapes=[
            pltpu.VMEM((NV, 6, 6, 6, 128), jnp.float32),
            pltpu.VMEM((1, 2, 32), jnp.int32),
            pltpu.VMEM((1, 2, 64), jnp.int32),
            pltpu.VMEM((6, 128), jnp.int32),
            pltpu.SemaphoreType.DMA((3,)),
            pltpu.SemaphoreType.DMA((NV,)),
        ],
        compiler_params=PARAMS,
        name="first_faces",
    )(*[pltpu.with_memory_space_constraint(value, pltpu.HBM) for value in args])


def volume_call(section, field, register, codes, face0, face2):
    def kernel(*refs):
        if section > 0:
            volume_kernel(section, *refs)
        else:
            volume_kernel(section, refs[0], None, *refs[1:])

    args = [field, codes, face0, face2] if section == 0 else [field, register, codes, face0, face2]
    outs = [vmem_out(FIELD), vmem_out(FACE0), vmem_out(FACE2)]
    return pl.pallas_call(
        kernel,
        out_shape=outs,
        in_specs=[VMEM_SPEC] * len(args),
        out_specs=[VMEM_SPEC] * len(outs),
        scratch_shapes=[
            pltpu.VMEM((6 * VROWS, 128), jnp.float32),
            pltpu.VMEM(FACE0, jnp.float32),
            pltpu.VMEM(FACE0, jnp.float32),
        ],
        compiler_params=PARAMS,
        cost_estimate=pl.CostEstimate(flops=10**7, bytes_accessed=4 * 10**6, transcendentals=0),
        name="volume",
    )(*map(in_vmem, args))


def surface_call(section, *args):
    last = section == len(RK_A) - 1

    def kernel(*refs):
        (last_kernel if last else surface_kernel)(section, *refs)

    if last:
        outs = [jax.ShapeDtypeStruct((NV, 6, 6, 6, 128), jnp.float32)] * 2
    else:
        outs = [vmem_out(FIELD), vmem_out(FIELD)] + face_outs()
    scratch = [
        pltpu.VMEM((2,) + FLOW_PACK, jnp.float32),
        pltpu.VMEM((2,) + SPAN_PACK, jnp.float32),
        pltpu.VMEM(FIELD, jnp.float32),
    ]
    if last:
        scratch += [pltpu.VMEM((NV, 6, 6, 6, 128), jnp.float32)] * 2
        scratch += [pltpu.SemaphoreType.DMA((2, 6))]
    return pl.pallas_call(
        kernel,
        out_shape=outs,
        in_specs=[VMEM_SPEC] * len(args),
        out_specs=[pl.BlockSpec(memory_space=pltpu.HBM) if last else VMEM_SPEC] * len(outs),
        scratch_shapes=scratch,
        compiler_params=PARAMS,
        name="surface",
    )(*map(in_vmem, args))


def swap(value, axis, crossing):
    length = lax.axis_size(axis)
    if crossing:
        pairs = [(i, (i + 1) % length if i % 2 else (i - 1) % length) for i in range(length)]
    else:
        pairs = [(i, i ^ 1) for i in range(length)]
    return lax.ppermute(value, axis, pairs)


def body(conserved, flow_lists, span_lists, face_source):
    field, codes, *faces = first_call(conserved, flow_lists, span_lists, face_source)
    register = None
    for section in range(len(RK_A)):
        face0, face2, flow_a, flow_b, span_a, span_b = faces
        rd = swap(span_b, "py", True)
        rc = swap(span_a, "py", False)
        rb = swap(flow_b, "px", True)
        ra = swap(flow_a, "px", False)
        base, near0, near2 = volume_call(section, field, register, codes, face0, face2)
        outs = surface_call(
            section, codes, field, base, face0, face2, near0, near2, ra, rb, rc, rd
        )
        if section == len(RK_A) - 1:
            return tuple(outs)
        field, register, *faces = outs


def solution(mesh):
    return jax.shard_map(
        body,
        mesh=mesh,
        in_specs=(
            P(None, None, None, None, ("px", "py")),
            P(("px", "py"), None, None),
            P(("px", "py"), None, None),
            P(None, ("px", "py")),
        ),
        out_specs=(
            P(None, None, None, None, ("px", "py")),
            P(None, None, None, None, ("px", "py")),
        ),
        check_vma=False,
    )
```

```python
import math

import jax
import jax.numpy as jnp
import numpy as np
from jax import lax
from jax.experimental import pallas as pl
from jax.experimental.pallas import tpu as pltpu
from jax.sharding import PartitionSpec as P

GAMMA = 1.4
VISCOSITY = 0.02
TIME_STEP = 0.01
RK_A = (
    0.0,
    -567301805773.0 / 1357537059087.0,
    -2404267990393.0 / 2016746695238.0,
    -3550918686646.0 / 2091501179385.0,
    -1275806237668.0 / 842570457699.0,
)
RK_B = (
    1432997174477.0 / 9575080441755.0,
    5161836677717.0 / 13612068292357.0,
    1720146321549.0 / 2090206949498.0,
    3134564353537.0 / 4481467310338.0,
    2277821191437.0 / 14882151754819.0,
)


def lobatto_tables():
    inner_node = math.sqrt(1.0 / 3.0 - 2.0 * math.sqrt(7.0) / 21.0)
    outer_node = math.sqrt(1.0 / 3.0 + 2.0 * math.sqrt(7.0) / 21.0)
    points = np.array([-1.0, -outer_node, -inner_node, inner_node, outer_node, 1.0])
    legendre = (63.0 * points**5 - 70.0 * points**3 + 15.0 * points) / 8.0
    weights = 2.0 / (30.0 * legendre * legendre)
    identity = np.eye(6)
    differences = points[:, None] - points[None, :] + identity
    barycentric = 1.0 / np.prod(differences, axis=1)
    matrix = barycentric[None, :] / barycentric[:, None] / differences
    matrix = matrix * (1.0 - identity)
    matrix = matrix - identity * np.sum(matrix, axis=1)[:, None]
    return matrix, weights


DM, WEIGHTS = lobatto_tables()
DM2 = DM @ DM
LIFT = 1.0 / WEIGHTS[0]
NV = 5
VROWS = 320
FIELD = (NV * VROWS, 128)
FACE0 = (2, 60, 8, 128)
FACE2 = (2, 55, 8, 128)
FLOW_PACK = (15, 8, 128)
SPAN_PACK = (23, 8, 128)
FLOW_FAR = (16, 8, 128)
SPAN_FAR = (24, 8, 128)
CODES = (10, 8, 128)
RECEIVED = 256
WALL = 512


def tile_at(ref, row):
    return ref[pl.ds(pl.multiple_of(row, 8), 8), :]


def put_tile(ref, row, value):
    ref[pl.ds(pl.multiple_of(row, 8), 8), :] = value


def line_at(ref, var, chunk, k):
    return ref[pl.ds(var * VROWS + chunk * 64 + k, 8, stride=8), :]


def put_line(ref, var, chunk, k, value):
    ref[pl.ds(var * VROWS + chunk * 64 + k, 8, stride=8), :] = value


def rows_loop(count, unroll, row):
    def step(n, carry):
        for u in range(unroll):
            row(n * unroll + u, carry)
        return carry

    if unroll == count:
        step(0, 0)
    else:
        lax.fori_loop(0, count // unroll, step, 0)


def span_place(q, chunk):
    return q * 4 + chunk if chunk < 4 else 40 + q // 2


def take_lanes(value, index):
    return jnp.take_along_axis(value, index, axis=1, mode="promise_in_bounds")


def even_odd(values):
    even = [values[m] + values[5 - m] for m in range(3)]
    odd = [values[m] - values[5 - m] for m in range(3)]
    return even, odd


def combine(coefficients, terms):
    total = None
    for coefficient, term in zip(coefficients, terms):
        part = float(coefficient) * term
        total = part if total is None else total + part
    return total


def end_derivatives(values):
    even, odd = even_odd(values)
    first = combine([(DM[0, m] + DM[0, 5 - m]) / 2 for m in range(3)], even)
    second = combine([(DM[0, m] - DM[0, 5 - m]) / 2 for m in range(3)], odd)
    return first + second, second - first


def jump_parts(low, high):
    total, difference = high + low, high - low
    even = [float((DM[i, 5] + DM[5 - i, 5]) / 2) * total for i in range(3)]
    odd = [float((DM[i, 5] - DM[5 - i, 5]) / 2) * difference for i in range(3)]
    return even, odd


def second_derivative(values, scale, jumps=None):
    even, odd = even_odd(values)
    result = [None] * 6
    for i in range(3):
        first = combine([scale * (DM2[i, m] + DM2[i, 5 - m]) / 2 for m in range(3)], even)
        second = combine([scale * (DM2[i, m] - DM2[i, 5 - m]) / 2 for m in range(3)], odd)
        if jumps is not None:
            first, second = first + jumps[0][i], second + jumps[1][i]
        result[i] = first + second
        result[5 - i] = first - second
    return result


def half_primitive(state):
    inverse = 1.0 / state[0]
    half = 0.5 * inverse
    velocity = [half * state[1], half * state[2], half * state[3]]
    kinetic = velocity[0] * state[1] + velocity[1] * state[2] + velocity[2] * state[3]
    pressure = (0.5 * (GAMMA - 1.0)) * (state[4] - kinetic)
    return [0.5 * state[0], velocity[0], velocity[1], velocity[2], pressure, half * state[4]]


def line_fluxes(nodes, direction):
    sums = [[None] * NV for _ in range(6)]

    def add(node, var, value, sign):
        old = sums[node][var]
        if old is None:
            sums[node][var] = value if sign > 0 else -value
        else:
            sums[node][var] = old + value if sign > 0 else old - value

    for i in range(6):
        for m in range(i + 1, 6):
            weight = float(2.0 * WEIGHTS[i] * DM[i, m])
            left, right = nodes[i], nodes[m]
            density, v0, v1, v2, pressure, specific = [left[n] + right[n] for n in range(6)]
            velocity = (v0, v1, v2)
            mass = (weight * density) * velocity[direction]
            scaled = weight * pressure
            flux = [mass, mass * v0, mass * v1, mass * v2, mass * specific + scaled * velocity[direction]]
            flux[1 + direction] = flux[1 + direction] + scaled
            for var in range(NV):
                add(i, var, flux[var], 1)
                add(m, var, flux[var], -1)
    return sums


def rusanov(left, right, direction, scale):
    def parts(state):
        inverse = 1.0 / state[0]
        velocity = state[1 + direction] * inverse
        kinetic = state[1] * state[1] + state[2] * state[2] + state[3] * state[3]
        pressure = (GAMMA - 1.0) * (state[4] - 0.5 * inverse * kinetic)
        speed = jnp.abs(velocity) + jnp.sqrt(GAMMA * pressure * inverse)
        flux = [state[1 + direction], state[1] * velocity, state[2] * velocity, state[3] * velocity]
        flux.append((state[4] + pressure) * velocity)
        flux[1 + direction] = flux[1 + direction] + pressure
        return flux, speed

    left_flux, left_speed = parts(left)
    right_flux, right_speed = parts(right)
    speed = jnp.maximum(left_speed, right_speed)
    return [
        (0.5 * scale) * ((left_flux[n] + right_flux[n]) - speed * (right[n] - left[n]))
        for n in range(NV)
    ]


def face_terms(low, high, direction):
    low_flux = rusanov(low[2], low[0], direction, TIME_STEP * LIFT)
    high_flux = rusanov(high[0], high[2], direction, TIME_STEP * LIFT)
    visc = TIME_STEP * 0.5 * VISCOSITY * LIFT
    ends_low, ends_high, jumps = [], [], []
    for n in range(NV):
        ends_low.append(low_flux[n] - visc * (low[3][n] - low[1][n]))
        ends_high.append(visc * (high[3][n] - high[1][n]) - high_flux[n])
        jumps.append(jump_parts(visc * (low[2][n] - low[0][n]), visc * (high[2][n] - high[0][n])))
    return ends_low, ends_high, jumps


def add_faces(values, terms, var):
    ends_low, ends_high, jumps = terms
    even, odd = jumps[var]
    result = [None] * 6
    for i in range(3):
        result[i] = values[i] + (even[i] + odd[i])
        result[5 - i] = values[5 - i] + (even[i] - odd[i])
    result[0] = result[0] + ends_low[var]
    result[5] = result[5] + ends_high[var]
    return result


def faces_flow(field, face0):
    def flow_row(j, carry):
        for v in range(NV):
            values = [tile_at(field, v * VROWS + i * 48 + j * 8) for i in range(6)]
            first, last = end_derivatives(values)
            face0[0, v * 6 + j] = values[0]
            face0[1, v * 6 + j] = values[5]
            face0[0, (NV + v) * 6 + j] = first
            face0[1, (NV + v) * 6 + j] = last
        return carry

    rows_loop(6, 6, flow_row)


def faces_span(field, face2):
    upper = lax.broadcasted_iota(jnp.int32, (8, 128), 0) >= 4
    for chunk in range(5):
        ends = [[None] * (2 * NV), [None] * (2 * NV)]
        for v in range(NV):
            values = [line_at(field, v, chunk, k) for k in range(6)]
            ends[0][v], ends[1][v] = values[0], values[5]
            ends[0][NV + v], ends[1][NV + v] = end_derivatives(values)
        for side in range(2):
            for q in range(2 * NV):
                face2[side, q * 5 + chunk] = ends[side][q]
                if chunk == 4 and q % 2:
                    shifted = pltpu.roll(ends[side][q], 4, 0)
                    face2[side, 50 + q // 2] = jnp.where(upper, shifted, ends[side][q - 1])


def pack_span(codes, side, face2, out):
    lane = lax.broadcasted_iota(jnp.int32, (8, 128), 1)
    index = codes[8 + side]
    rows = [q * 5 + chunk for q in range(2 * NV) for chunk in range(4)] + list(range(50, 55))
    for t in range(23):
        packed = take_lanes(face2[side, rows[t]], index)
        if 23 + t < 45:
            packed = jnp.where(lane >= 64, take_lanes(face2[side, rows[23 + t]], index), packed)
        out[t] = packed


def pack_flow(codes, side, face0, out):
    lane = lax.broadcasted_iota(jnp.int32, (8, 128), 1)
    index = codes[6 + side]
    for t in range(15):
        packed = take_lanes(face0[side, t], index)
        for g in range(1, 4):
            packed = jnp.where(lane >= 32 * g, take_lanes(face0[side, 15 * g + t], index), packed)
        out[t] = packed


def far_faces(field, codes, face2, span_b):
    faces_span(field, face2)
    pack_span(codes, lax.axis_index("py") & 1, face2, span_b)


def near_kernel(field, codes, face2, face0, flow_a, flow_b, span_a):
    flow_odd, span_odd = lax.axis_index("px") & 1, lax.axis_index("py") & 1
    faces_flow(field, face0)
    pack_span(codes, 1 - span_odd, face2, span_a)
    pack_flow(codes, flow_odd, face0, flow_b)
    pack_flow(codes, 1 - flow_odd, face0, flow_a)


def first_kernel(
    conserved, flow_lists, span_lists, face_source, field, codes, face2, span_b,
    state, flow_rows, span_rows, columns, list_sems, state_sems,
):
    copies = [
        pltpu.make_async_copy(source, target, list_sems.at[n])
        for n, (source, target) in enumerate(
            ((flow_lists, flow_rows), (span_lists, span_rows), (face_source, columns))
        )
    ]
    copies += [pltpu.make_async_copy(conserved.at[v], state.at[v], state_sems.at[v]) for v in range(NV)]
    for copy in copies:
        copy.start()
    for copy in copies[:3]:
        copy.wait()
    for side in range(6):
        column = columns[pl.ds(side, 1), :]
        mask = 31 if side < 2 else 63
        offset = 768 if side < 2 else 832
        code = jnp.where(
            column < 768,
            column & 127,
            jnp.where(column < 960, ((column - offset) & mask) + RECEIVED, WALL),
        )
        codes[side] = jnp.broadcast_to(code, (8, 128))
    for side in range(2):
        flow_row = jnp.concatenate([flow_rows[0, pl.ds(side, 1), :]] * 4, axis=1)
        span_row = jnp.concatenate([span_rows[0, pl.ds(side, 1), :]] * 2, axis=1)
        codes[6 + side] = jnp.broadcast_to(flow_row, (8, 128))
        codes[8 + side] = jnp.broadcast_to(span_row, (8, 128))
    for v in range(NV):
        copies[3 + v].wait()
        for i in range(6):
            for j in range(6):
                field[pl.ds(v * VROWS + i * 48 + j * 8, 6), :] = state[v, i, j]
    far_faces(field, codes, face2, span_b)


def volume_kernel(
    section, field, register, codes, face0, face2, base, near0, near2, prims, face1, near1
):
    volume_primitives(field, prims)
    wall_faces(field, face1)
    volume_flow(section, field, register, codes, base, prims, face1, near1)
    volume_wall(field, codes, base, prims, face1, near1, face0, near0)
    volume_span(field, codes, base, prims, face2, near2)


def take_local(codes, first_side, face, near, tiles, t):
    for side in range(2):
        index = codes[first_side + side] & 127
        for q in range(2 * NV):
            near[side, q * tiles + t] = take_lanes(face[1 - side, q * tiles + t], index)


def volume_primitives(field, prims):
    def primitives(n, carry):
        for u in range(4):
            row = (n * 4 + u) * 8
            values = half_primitive([tile_at(field, v * VROWS + row) for v in range(NV)])
            for q in range(6):
                put_tile(prims, q * VROWS + row, values[q])
        return carry

    rows_loop(9, 9, primitives)


def volume_flow(section, field, register, codes, base, prims, face1, near1):
    step = TIME_STEP

    def flow_row(j, carry):
        row = j * 8
        nodes = [[tile_at(prims, q * VROWS + i * 48 + row) for q in range(6)] for i in range(6)]
        sums = line_fluxes(nodes, 0)
        for v in range(NV):
            line = [tile_at(field, v * VROWS + i * 48 + row) for i in range(6)]
            second = second_derivative(line, step * VISCOSITY)
            for i in range(6):
                value = second[i] - float(step / WEIGHTS[i]) * sums[i][v]
                if section > 0:
                    value = value + RK_A[section] * tile_at(register, v * VROWS + i * 48 + row)
                put_tile(base, v * VROWS + i * 48 + row, value)
        take_local(codes, 2, face1, near1, 6, j)
        return carry

    lax.fori_loop(0, 6, flow_row, 0)


def wall_faces(field, face1):
    def wall_row(i, carry):
        for v in range(NV):
            values = [tile_at(field, v * VROWS + i * 48 + j * 8) for j in range(6)]
            first, last = end_derivatives(values)
            face1[0, v * 6 + i] = values[0]
            face1[1, v * 6 + i] = values[5]
            face1[0, (NV + v) * 6 + i] = first
            face1[1, (NV + v) * 6 + i] = last
        return carry

    rows_loop(6, 6, wall_row)


def volume_wall(field, codes, base, prims, face1, near1, face0, near0):
    step = TIME_STEP

    def wall_row(i, carry):
        row = i * 48
        nodes = [[tile_at(prims, q * VROWS + row + j * 8) for q in range(6)] for j in range(6)]
        sums = line_fluxes(nodes, 1)
        low, high = sides(codes, 2, face1, near1, 6, i)
        terms = face_terms(low, high, 1)
        for v in range(NV):
            line = [tile_at(field, v * VROWS + row + j * 8) for j in range(6)]
            second = second_derivative(line, step * VISCOSITY, terms[2][v])
            values = [second[j] - float(step / WEIGHTS[j]) * sums[j][v] for j in range(6)]
            values[0] = values[0] + terms[0][v]
            values[5] = values[5] + terms[1][v]
            for j in range(6):
                where = v * VROWS + row + j * 8
                put_tile(base, where, tile_at(base, where) + values[j])
        take_local(codes, 0, face0, near0, 6, i)
        return carry

    lax.fori_loop(0, 6, wall_row, 0)


def volume_span(field, codes, base, prims, face2, near2):
    step = TIME_STEP

    def span_row(chunk, carry):
        nodes = [[line_at(prims, q, chunk, k) for q in range(6)] for k in range(6)]
        sums = line_fluxes(nodes, 2)
        for v in range(NV):
            line = [line_at(field, v, chunk, k) for k in range(6)]
            second = second_derivative(line, step * VISCOSITY)
            for k in range(6):
                value = second[k] - float(step / WEIGHTS[k]) * sums[k][v]
                put_line(base, v, chunk, k, line_at(base, v, chunk, k) + value)
        take_local(codes, 4, face2, near2, 5, chunk)
        return carry

    lax.fori_loop(0, 5, span_row, 0)


def surface_update(
    section, last, codes, field, base, face0, face2, near0, near2, received,
    new_field, new_register, got0, got2, work, *staging,
):
    flow_a, flow_b, span_a, span_b = received
    flow_odd, span_odd = lax.axis_index("px") & 1, lax.axis_index("py") & 1
    got2[1 - span_odd] = span_a[...]
    got2[span_odd] = span_b[pl.ds(0, 23)]
    got0[1 - flow_odd] = flow_a[...]
    got0[flow_odd] = flow_b[pl.ds(0, 15)]
    surface_span(codes, base, face2, near2, got2, work)
    surface_flow(
        section, last, codes, field, face0, near0, got0, new_field, new_register, work, *staging
    )


def sides(codes, first_side, own, near, tiles, t, got=None, groups=1):
    result = []
    for side in range(2):
        code = codes[first_side + side]
        wall = code >= WALL
        received = (code & RECEIVED) != 0
        own_values, other_values = [], []
        for q in range(2 * NV):
            row = q * tiles + t
            own_value = own[side, row]
            other_value = near[side, row]
            if got is not None:
                place, share = (span_place(q, t), 23) if groups == 2 else (row, 15)
                index = (code + (128 // groups) * (place // share)) & 127
                taken = take_lanes(got[side, place % share], index)
                if groups == 2 and t == 4 and q % 2:
                    taken = pltpu.roll(taken, 4, 0)
                other_value = jnp.where(received, taken, other_value)
            mirrored = -own_value if 1 <= q <= 3 else own_value
            own_values.append(own_value)
            other_values.append(jnp.where(wall, mirrored, other_value))
        result.append((own_values[:NV], own_values[NV:], other_values[:NV], other_values[NV:]))
    return result


def surface_span(codes, base, face2, near2, got2, work):
    def span_row(chunk, carry):
        low, high = sides(codes, 4, face2, near2, 5, chunk, got2, 2)
        terms = face_terms(low, high, 2)
        for v in range(NV):
            values = [line_at(base, v, chunk, k) for k in range(6)]
            values = add_faces(values, terms, v)
            for k in range(6):
                put_line(work, v, chunk, k, values[k])
        return carry

    rows_loop(5, 5, span_row)


def surface_flow(
    section, last, codes, field, face0, near0, got0, new_field, new_register, work,
    out_state=None, out_register=None, sems=None,
):
    copies = []

    def flow_row(j, carry):
        low, high = sides(codes, 0, face0, near0, 6, j, got0, 4)
        terms = face_terms(low, high, 0)
        for v in range(NV):
            rows = [v * VROWS + i * 48 + j * 8 for i in range(6)]
            values = add_faces([tile_at(work, row) for row in rows], terms, v)
            for i in range(6):
                updated = tile_at(field, rows[i]) + RK_B[section] * values[i]
                if last:
                    out_state[v, i, j] = updated[:6]
                    out_register[v, i, j] = values[i][:6]
                else:
                    put_tile(new_field, rows[i], updated)
                    put_tile(new_register, rows[i], values[i])
        if last:
            for n, (source, target) in enumerate(((out_state, new_field), (out_register, new_register))):
                copy = pltpu.make_async_copy(source.at[:, :, j], target.at[:, :, j], sems.at[n, j])
                copy.start()
                copies.append(copy)
        return carry

    rows_loop(6, 6, flow_row)
    for copy in copies:
        copy.wait()


def surface_kernel(
    section, codes, field, base, face0, face2, near0, near2, ra, rb, rc, rd,
    new_field, new_register, new_face2, span_b, got0, got2, work,
):
    surface_update(
        section, False, codes, field, base, face0, face2, near0, near2, (ra, rb, rc, rd),
        new_field, new_register, got0, got2, work,
    )
    far_faces(new_field, codes, new_face2, span_b)


def last_kernel(
    section, codes, field, base, face0, face2, near0, near2, ra, rb, rc, rd,
    advanced, register, got0, got2, work, *staging,
):
    surface_update(
        section, True, codes, field, base, face0, face2, near0, near2, (ra, rb, rc, rd),
        advanced, register, got0, got2, work, *staging,
    )


def in_vmem(value):
    return pltpu.with_memory_space_constraint(value, pltpu.VMEM)


VMEM_SPEC = pl.BlockSpec(memory_space=pltpu.VMEM)
PARAMS = pltpu.CompilerParams(vmem_limit_bytes=32 * 1024 * 1024)


def vmem_out(shape, dtype=jnp.float32):
    return pltpu.VMEM(shape, dtype)


def near_call(field, codes, face2):
    shapes = (FACE0, FLOW_PACK, FLOW_FAR, SPAN_PACK)
    return pl.pallas_call(
        near_kernel,
        out_shape=[vmem_out(shape) for shape in shapes],
        in_specs=[VMEM_SPEC] * 3,
        out_specs=[VMEM_SPEC] * len(shapes),
        compiler_params=PARAMS,
        cost_estimate=pl.CostEstimate(flops=10**6, bytes_accessed=10**6, transcendentals=0),
        name="near_faces",
    )(*map(in_vmem, (field, codes, face2)))


def first_call(*args):
    outs = [vmem_out(FIELD), vmem_out(CODES, jnp.int32), vmem_out(FACE2), vmem_out(SPAN_FAR)]
    return pl.pallas_call(
        first_kernel,
        out_shape=outs,
        in_specs=[pl.BlockSpec(memory_space=pltpu.HBM)] * len(args),
        out_specs=[VMEM_SPEC] * len(outs),
        scratch_shapes=[
            pltpu.VMEM((NV, 6, 6, 6, 128), jnp.float32),
            pltpu.VMEM((1, 2, 32), jnp.int32),
            pltpu.VMEM((1, 2, 64), jnp.int32),
            pltpu.VMEM((6, 128), jnp.int32),
            pltpu.SemaphoreType.DMA((3,)),
            pltpu.SemaphoreType.DMA((NV,)),
        ],
        compiler_params=PARAMS,
        name="first_faces",
    )(*[pltpu.with_memory_space_constraint(value, pltpu.HBM) for value in args])


def volume_call(section, field, register, codes, face0, face2):
    def kernel(*refs):
        if section > 0:
            volume_kernel(section, *refs)
        else:
            volume_kernel(section, refs[0], None, *refs[1:])

    args = [field, codes, face0, face2] if section == 0 else [field, register, codes, face0, face2]
    outs = [vmem_out(FIELD), vmem_out(FACE0), vmem_out(FACE2)]
    return pl.pallas_call(
        kernel,
        out_shape=outs,
        in_specs=[VMEM_SPEC] * len(args),
        out_specs=[VMEM_SPEC] * len(outs),
        scratch_shapes=[
            pltpu.VMEM((6 * VROWS, 128), jnp.float32),
            pltpu.VMEM(FACE0, jnp.float32),
            pltpu.VMEM(FACE0, jnp.float32),
        ],
        compiler_params=PARAMS,
        cost_estimate=pl.CostEstimate(flops=10**4, bytes_accessed=10**4, transcendentals=0),
        name="volume",
    )(*map(in_vmem, args))


def surface_call(section, *args):
    last = section == len(RK_A) - 1

    def kernel(*refs):
        (last_kernel if last else surface_kernel)(section, *refs)

    if last:
        outs = [jax.ShapeDtypeStruct((NV, 6, 6, 6, 128), jnp.float32)] * 2
    else:
        outs = [vmem_out(FIELD), vmem_out(FIELD), vmem_out(FACE2), vmem_out(SPAN_FAR)]
    scratch = [
        pltpu.VMEM((2,) + FLOW_PACK, jnp.float32),
        pltpu.VMEM((2,) + SPAN_PACK, jnp.float32),
        pltpu.VMEM(FIELD, jnp.float32),
    ]
    if last:
        scratch += [pltpu.VMEM((NV, 6, 6, 6, 128), jnp.float32)] * 2
        scratch += [pltpu.SemaphoreType.DMA((2, 6))]
    return pl.pallas_call(
        kernel,
        out_shape=outs,
        in_specs=[VMEM_SPEC] * len(args),
        out_specs=[pl.BlockSpec(memory_space=pltpu.HBM) if last else VMEM_SPEC] * len(outs),
        scratch_shapes=scratch,
        compiler_params=PARAMS,
        name="surface",
    )(*map(in_vmem, args))


def swap(value, axis, crossing):
    length = lax.axis_size(axis)
    if crossing:
        pairs = [(i, (i + 1) % length if i % 2 else (i - 1) % length) for i in range(length)]
    else:
        pairs = [(i, i ^ 1) for i in range(length)]
    return lax.ppermute(value, axis, pairs)


def body(conserved, flow_lists, span_lists, face_source):
    field, codes, face2, span_b = first_call(conserved, flow_lists, span_lists, face_source)
    register = None
    for section in range(len(RK_A)):
        rd = swap(span_b, "py", True)
        face0, flow_a, flow_b, span_a = near_call(field, codes, face2)
        rc = swap(span_a, "py", False)
        rb = swap(flow_b, "px", True)
        ra = swap(flow_a, "px", False)
        base, near0, near2 = volume_call(section, field, register, codes, face0, face2)
        outs = surface_call(
            section, codes, field, base, face0, face2, near0, near2, ra, rb, rc, rd
        )
        if section == len(RK_A) - 1:
            return tuple(outs)
        field, register, face2, span_b = outs


def solution(mesh):
    return jax.shard_map(
        body,
        mesh=mesh,
        in_specs=(
            P(None, None, None, None, ("px", "py")),
            P(("px", "py"), None, None),
            P(("px", "py"), None, None),
            P(None, ("px", "py")),
        ),
        out_specs=(
            P(None, None, None, None, ("px", "py")),
            P(None, None, None, None, ("px", "py")),
        ),
        check_vma=False,
    )
```
